256 devices in a mesh: section: 4 (over z_lo), dp: 64 (over z_hi, y, x, core).
Axes of the slice: x: 4, y: 4, z: 8 (z_hi: 2, z_lo: 4; z = z_hi * 4 + z_lo), core: 2. Of those that a mesh axis runs over, the one named last changes fastest.
Arguments:
- images: bfloat16 [4, 64, 16, 16, 320], P(None, 'dp'), may hold values from -6 to 6
- cotangent: bfloat16 [4, 64, 16, 16, 320], P(None, 'dp'), may hold values from -6 to 6
- heights: int32 [4], replicated, may hold values from 8 to 16, as said below
- dw_kernel: float32 [2, 4, 7, 7, 320], P(None, 'section'), may hold values from -0.875 to 0.875
- dw_bias: float32 [2, 4, 320], P(None, 'section'), may hold values from -1 to 1
- norm_gain: float32 [2, 4, 320], P(None, 'section'), may hold values from 0.5 to 1.5
- norm_bias: float32 [2, 4, 320], P(None, 'section'), may hold values from -3 to 3
- up_weight: bfloat16 [2, 4, 320, 1280], P(None, 'section'), may hold values from -0.3125 to 0.3125
- up_bias: float32 [2, 4, 1280], P(None, 'section'), may hold values from -3 to 3
- down_weight: bfloat16 [2, 4, 1280, 320], P(None, 'section'), may hold values from -0.15625 to 0.15625
- down_bias: float32 [2, 4, 320], P(None, 'section'), may hold values from -3 to 3
- layer_scale: float32 [2, 4, 320], P(None, 'section'), may hold values from 0.1 to 1
Outputs:
- grad_dw_kernel: float32 [2, 4, 7, 7, 320], P(None, 'section')
- grad_dw_bias: float32 [2, 4, 320], P(None, 'section')
- grad_norm_gain: float32 [2, 4, 320], P(None, 'section')
- grad_norm_bias: float32 [2, 4, 320], P(None, 'section')
- grad_up_weight: bfloat16 [2, 4, 320, 1280], P(None, 'section')
- grad_up_bias: float32 [2, 4, 1280], P(None, 'section')
- grad_down_weight: bfloat16 [2, 4, 1280, 320], P(None, 'section')
- grad_down_bias: float32 [2, 4, 320], P(None, 'section')
- grad_layer_scale: float32 [2, 4, 320], P(None, 'section')
The draws below stay inside these ranges and needn't reach their ends.
Inputs may be any that keep to these rules, and one draw needn't show every extreme that they name: heights[m] is one of 8, 12 and 16; some micro-batch has 16.
All inputs are finite; a program needn't handle non-finite values.
Results may differ from the reference program's by a relative error of at most 0.025.
Values may be sent and summed in bfloat16 or wider, within the bound.
A program may use at most 128 MiB of HBM per device.

```python
import math
import jax
import jax.numpy as jnp
from jax import lax

C = 320
HID = 1280
SIDE = 16
MICRO = 4
LOOPS = 2
IMGS = 64
N_SECTION = 4
N_DP = 64


def draw_heights(key, part):
    first, second = jax.random.split(jax.random.fold_in(key, 11))
    levels = jax.random.randint(first, (MICRO,), 2, 5) * (SIDE // 4)
    spot = jax.random.randint(second, (), 0, MICRO)
    return jnp.where(jnp.arange(MICRO) == spot, SIDE, levels).astype(jnp.int32)


def block_scale(key, extent, shards, least, high):
    gain, own = 1.0, jax.random.fold_in(key, 6)
    for axis_at, blocks in shards:
        draws = jnp.exp(jax.random.uniform(jax.random.fold_in(own, axis_at), (blocks,), jnp.float32, least / len(shards), high / len(shards)))
        gain = gain * jnp.repeat(draws, extent[axis_at] // blocks).reshape([-1 if axis == axis_at else 1 for axis in range(len(extent))])
    return gain


def normal_values(own_key, dims, scale, bound, cuts=(), held_as=jnp.bfloat16):
    values = jax.random.normal(own_key, dims, jnp.float32) * scale
    if len(cuts) > 0:
        values = block_scale(own_key, dims, cuts, -0.22, 0.18) * values
    return jnp.clip(values, min=-bound, max=bound).astype(held_as)


def setup_inputs(seed: int = 0) -> dict:
    key_of = jax.random.split(jax.random.key(seed), 13)
    return {
        "images": normal_values(key_of[0], (MICRO, IMGS, SIDE, SIDE, C), 1.0, 6.0, ((1, 64),)),
        "cotangent": normal_values(key_of[1], (MICRO, IMGS, SIDE, SIDE, C), 1.0, 6.0, ((1, 64),)),
        "heights": draw_heights(jax.random.fold_in(key_of[12], 71), 0),
        "dw_kernel": normal_values(key_of[3], (LOOPS, N_SECTION, 7, 7, C), 49 ** -0.5, 0.875, ((1, 4),), jnp.float32),
        "dw_bias": jnp.clip(jax.random.uniform(key_of[4], (LOOPS, N_SECTION, C), jnp.float32, -1.0, 1.0) * block_scale(key_of[4], (LOOPS, N_SECTION, C), ((1, 4),), -0.4, 0.0), -1.0, 1.0),
        "norm_gain": jnp.clip(1.0 + 0.1 * jax.random.normal(key_of[5], (LOOPS, N_SECTION, C), jnp.float32), 0.5, 1.5),
        "norm_bias": normal_values(key_of[6], (LOOPS, N_SECTION, C), 0.5, 3.0, ((1, 4),), jnp.float32),
        "up_weight": normal_values(key_of[7], (LOOPS, N_SECTION, C, HID), C ** -0.5, 0.3125, ((1, 4),)),
        "up_bias": normal_values(key_of[8], (LOOPS, N_SECTION, HID), 0.5, 3.0, ((1, 4),), jnp.float32),
        "down_weight": normal_values(key_of[9], (LOOPS, N_SECTION, HID, C), HID ** -0.5, 0.15625, ((1, 4),)),
        "down_bias": normal_values(key_of[10], (LOOPS, N_SECTION, C), 0.5, 3.0, ((1, 4),), jnp.float32),
        "layer_scale": jnp.clip(jnp.exp(math.log(1.0) - 2.3025851 * jax.random.uniform(key_of[11], (LOOPS, N_SECTION, C), jnp.float32) ** block_scale(key_of[11], (LOOPS, N_SECTION, C), ((1, 4),), -0.2, 0.2)), 0.1, 1.0),
    }


def make_window(height, side):
    rows = lax.iota(jnp.int32, side)
    inside = (rows < height).astype(jnp.float32)
    return inside[:, None] * inside[None, :]

def block_apply(params, inputs, window):
    dw_kernel, dw_bias, norm_gain, norm_bias, up_weight, up_bias, down_weight, down_bias, layer_scale = params
    side = inputs.shape[0]
    width = inputs.shape[2]
    widened = inputs.astype(jnp.float32)
    padded = jnp.pad(widened, ((3, 3), (3, 3), (0, 0)))
    mixed = jnp.zeros_like(widened) + dw_bias
    for row_off in range(7):
        for col_off in range(7):
            mixed = mixed + padded[row_off:row_off + side, col_off:col_off + side] * dw_kernel[row_off, col_off]
    center = lax.optimization_barrier(jnp.mean(mixed, axis=-1, keepdims=True))
    spread = lax.optimization_barrier(jnp.mean((mixed - center) ** 2, axis=-1, keepdims=True))
    normed = ((mixed - center) * lax.rsqrt(spread + 1e-06) * norm_gain + norm_bias).astype(jnp.bfloat16)
    flat = normed.reshape(side * side, width)
    hidden = jnp.dot(flat, up_weight, preferred_element_type=jnp.float32) + up_bias
    active = jax.nn.gelu(hidden, approximate=True).astype(jnp.bfloat16)
    projected = jnp.dot(active, down_weight, preferred_element_type=jnp.float32) + down_bias
    result = (widened + layer_scale * projected.reshape(side, side, width)) * window[:, :, None]
    return result.astype(jnp.bfloat16)

def reference(images, cotangent, heights, dw_kernel, dw_bias, norm_gain, norm_bias, up_weight, up_bias, down_weight, down_bias, layer_scale):
    weights = (dw_kernel, dw_bias, norm_gain, norm_bias, up_weight, up_bias, down_weight, down_bias, layer_scale)
    flat_params = tuple((a.reshape((LOOPS * N_SECTION,) + a.shape[2:]) for a in weights))

    def one_image(totals, index):
        micro = index // N_DP
        image = index % N_DP
        window = make_window(heights[micro], SIDE)
        start = (images[micro, image].astype(jnp.float32) * window[:, :, None]).astype(jnp.bfloat16)

        def forward(state, params):
            return (block_apply(params, state, window), state)
        final_state, stored = lax.scan(forward, start, flat_params)

        def backward(grad, pair):
            params, inputs = pair
            unused, pullback = jax.vjp(lambda p, v: block_apply(p, v, window), params, inputs)
            dparams, dinputs = pullback(grad)
            return (dinputs, tuple((g.astype(jnp.float32) for g in dparams)))
        unused_grad, grads = lax.scan(backward, cotangent[micro, image], (flat_params, stored), reverse=True)
        return (tuple((t + g for t, g in zip(totals, grads))), None)
    zeros = tuple((jnp.zeros(a.shape, jnp.float32) for a in flat_params))
    totals, unused_out = lax.scan(one_image, zeros, jnp.arange(MICRO * N_DP, dtype=jnp.int32))
    shaped = [t.reshape(w.shape) for t, w in zip(totals, weights)]
    shaped[4] = shaped[4].astype(jnp.bfloat16)
    shaped[6] = shaped[6].astype(jnp.bfloat16)
    return (shaped[0], shaped[1], shaped[2], shaped[3], shaped[4], shaped[5], shaped[6], shaped[7], shaped[8])
```

```python
import functools
import jax
import jax.numpy as jnp
from jax import lax
from jax.experimental import pallas as pl
from jax.experimental.pallas import tpu as pltpu
from jax.sharding import PartitionSpec as P

C, HID, SIDE, NB = 320, 1280, 16, 8
CP = 384
CELLS = SIDE * SIDE
ROWS = 6656
BF, F32 = jnp.bfloat16, jnp.float32
K0, K1 = 0.7978845608028654, 0.044715
T_LANES = (((1,), (1,)), ((), ()))
T_ROWS = (((0,), (0,)), ((), ()))


def dot(a, b, dims=(((1,), (0,)), ((), ()))):
    return lax.dot_general(a, b, dims, preferred_element_type=F32)


def lane_tile(t):
    return pl.ds(pl.multiple_of(t * 128, 128), 128)


def conv_forward(pad_ref, small_ref, b, out_ref):
    def tile(t, _):
        lanes = lane_tile(t)
        for half in range(2):
            bias = jnp.broadcast_to(small_ref[b, 49:50, lanes], (8, 128))
            acc = [bias] * SIDE
            for dj in range(7):
                taps = [jnp.broadcast_to(small_ref[b, pl.ds(dr * 7 + dj, 1), lanes], (8, 128)) for dr in range(7)]
                for r in range(SIDE):
                    x = pad_ref[r, pl.ds(8 * half + 5 + dj, 8), lanes]
                    for dr in range(7):
                        i = r - dr + 3
                        if 0 <= i < SIDE:
                            acc[i] = acc[i] + x * taps[dr]
            for i in range(SIDE):
                out_ref[i, pl.ds(8 * half, 8), lanes] = acc[i]
        return 0

    lax.fori_loop(0, 3, tile, 0)


def conv_backward(gpad_ref, x_ref, small_ref, b, dx_ref, dk_ref):
    def tile(t, _):
        lanes = lane_tile(t)
        for half in range(2):
            xs = [x_ref[i, pl.ds(8 * half, 8), lanes] for i in range(SIDE)]
            acc = [jnp.zeros((8, 128), F32)] * SIDE
            for dj in range(7):
                taps = [jnp.broadcast_to(small_ref[b, pl.ds(dr * 7 + dj, 1), lanes], (8, 128)) for dr in range(7)]
                dks = [None] * 7
                for r in range(SIDE):
                    g = gpad_ref[r, pl.ds(8 * half + 11 - dj, 8), lanes]
                    for dr in range(7):
                        i = r + dr - 3
                        if 0 <= i < SIDE:
                            acc[i] = acc[i] + g * taps[dr]
                            p = g * xs[i]
                            dks[dr] = p if dks[dr] is None else dks[dr] + p
                for dr in range(7):
                    if half == 0:
                        dk_ref[dr * 7 + dj, :, lanes] = dks[dr]
                    else:
                        dk_ref[dr * 7 + dj, :, lanes] += dks[dr]
            for i in range(SIDE):
                dx_ref[i, pl.ds(8 * half, 8), lanes] = acc[i]
        return 0

    lax.fori_loop(0, 3, tile, 0)


def small_row(small_ref, b, row):
    return small_ref[b, row : row + 1, 0:C]


def up_bias_chunk(small_ref, b, n):
    parts = []
    for t in (2 * n, 2 * n + 1):
        parts.append(small_ref[b, 54 + t // 3 : 55 + t // 3, (t % 3) * 128 : (t % 3 + 1) * 128])
    return jnp.concatenate(parts, axis=1)


def window_of(h):
    cell = lax.broadcasted_iota(jnp.int32, (CELLS, 1), 0)
    return ((cell // SIDE < h) & (cell % SIDE < h)).astype(F32)


def block_forward(b, h, w_ref, small_ref, v_ref, pad_ref, mix_ref, act_ref, slope_ref, xhat_ref, inv_ref, proj_ref):
    v = v_ref[b].astype(F32)
    pad_ref[:, 8:24, 0:C] = v.reshape(SIDE, SIDE, C)
    conv_forward(pad_ref, small_ref, b, mix_ref)
    mixed = mix_ref[:, :, 0:C].reshape(CELLS, C)
    center = jnp.sum(mixed, axis=1, keepdims=True) * (1.0 / C)
    mixed = mixed - center
    inv = lax.rsqrt(jnp.sum(mixed * mixed, axis=1, keepdims=True) * (1.0 / C) + 1e-6)
    xhat = mixed * inv
    xhat_ref[b] = xhat
    inv_ref[b] = inv
    normed = (xhat * small_row(small_ref, b, 50) + small_row(small_ref, b, 51)).astype(BF)
    proj = jnp.broadcast_to(small_row(small_ref, b, 52), (CELLS, C))
    for n in range(5):
        cols = slice(256 * n, 256 * n + 256)
        u = dot(normed, w_ref[b, 0:C, cols]) + up_bias_chunk(small_ref, b, n)
        uu = u * u
        t = jnp.tanh(u * (K0 + (K0 * K1) * uu))
        lift = 0.5 + 0.5 * t
        act = (u * lift).astype(BF)
        slope = lift + (u * (0.5 - 0.5 * t * t)) * (K0 + (3 * K0 * K1) * uu)
        act_ref[b, :, cols] = act
        slope_ref[b, :, cols] = slope.astype(BF)
        proj = proj + dot(act, w_ref[b, C : 2 * C, cols], T_LANES)
    proj_ref[b] = proj.astype(BF)
    out = (v + small_row(small_ref, b, 53) * proj) * window_of(h)
    return out.astype(BF)


def block_backward(b, h, g, w_ref, small_ref, v_ref, pad_ref, mix_ref, x_ref, act_ref, slope_ref, xhat_ref, inv_ref, proj_ref, dk_ref, sg_ref, out_ref):
    g = g * window_of(h)
    sg_ref[53:54, 0:C] = jnp.sum(g * proj_ref[b].astype(F32), axis=0, keepdims=True)
    dproj = g * small_row(small_ref, b, 53)
    sg_ref[52:53, 0:C] = jnp.sum(dproj, axis=0, keepdims=True)
    dproj = dproj.astype(BF)
    xhat = xhat_ref[b]
    gain = small_row(small_ref, b, 50)
    normed = (xhat * gain + small_row(small_ref, b, 51)).astype(BF)
    dnormed = None
    for n in range(5):
        cols = slice(256 * n, 256 * n + 256)
        dact = dot(dproj, w_ref[b, C : 2 * C, cols])
        dhid = dact * slope_ref[b, :, cols].astype(F32)
        bias = jnp.sum(dhid, axis=0, keepdims=True)
        dhid = dhid.astype(BF)
        part = dot(dhid, w_ref[b, 0:C, cols], T_LANES)
        dnormed = part if dnormed is None else dnormed + part
        dup = dot(normed, dhid, T_ROWS).astype(BF)
        ddown = dot(dproj, act_ref[b, :, cols], T_ROWS).astype(BF)
        for k in range(2):
            t = 2 * n + k
            lanes = slice(128 * k, 128 * k + 128)
            out_ref[b, 320 * t : 320 * t + 320, :] = dup[:, lanes]
            out_ref[b, 3200 + 320 * t : 3520 + 320 * t, :] = ddown[:, lanes]
            sg_ref[54 + t // 3 : 55 + t // 3, (t % 3) * 128 : (t % 3 + 1) * 128] = bias[:, lanes]
    sg_ref[50:51, 0:C] = jnp.sum(dnormed * xhat, axis=0, keepdims=True)
    sg_ref[51:52, 0:C] = jnp.sum(dnormed, axis=0, keepdims=True)
    dxhat = dnormed * gain
    m0 = jnp.sum(dxhat, axis=1, keepdims=True) * (1.0 / C)
    m1 = jnp.sum(dxhat * xhat, axis=1, keepdims=True) * (1.0 / C)
    dmixed = inv_ref[b] * (dxhat - m0 - xhat * m1)
    sg_ref[49:50, 0:C] = jnp.sum(dmixed, axis=0, keepdims=True)
    pad_ref[:, 8:24, 0:C] = dmixed.reshape(SIDE, SIDE, C)
    x_ref[:, :, 0:C] = v_ref[b].astype(F32).reshape(SIDE, SIDE, C)
    conv_backward(pad_ref, x_ref, small_ref, b, mix_ref, dk_ref)
    sg_ref[0:49, :] = jnp.sum(dk_ref[...], axis=1)
    for j in range(3):
        out_ref[b, 6400 + 64 * j : 6464 + 64 * j, :] = sg_ref[:, 128 * j : 128 * j + 128].astype(BF)
    return (g + mix_ref[:, :, 0:C].reshape(CELLS, C)).astype(BF).astype(F32)


def clear(ref):
    ref[...] = jnp.zeros(ref.shape, ref.dtype)


def compute_kernel(h_ref, image_ref, cot_ref, w_ref, small_ref, out_ref, v_ref, pad_ref, mix_ref, x_ref, act_ref, slope_ref, xhat_ref, inv_ref, proj_ref, dk_ref, sg_ref, g_ref):
    h = h_ref[0]
    clear(pad_ref)
    clear(x_ref)
    clear(sg_ref)
    v_ref[0] = (image_ref[...].astype(F32) * window_of(h)).astype(BF)

    def forward(b, _):
        v_ref[b + 1] = block_forward(b, h, w_ref, small_ref, v_ref, pad_ref, mix_ref, act_ref, slope_ref, xhat_ref, inv_ref, proj_ref)
        return 0

    lax.fori_loop(0, NB, forward, 0)
    g_ref[...] = cot_ref[...].astype(F32)

    def backward(i, _):
        b = NB - 1 - i
        out_ref[b, 6592:6656, :] = jnp.zeros((64, 128), BF)
        g_ref[...] = block_backward(b, h, g_ref[...], w_ref, small_ref, v_ref, pad_ref, mix_ref, x_ref, act_ref, slope_ref, xhat_ref, inv_ref, proj_ref, dk_ref, sg_ref, out_ref)
        return 0

    lax.fori_loop(0, NB, backward, 0)


def compute_scratch():
    return [
        pltpu.VMEM((NB + 1, CELLS, C), BF),
        pltpu.VMEM((SIDE, 32, CP), F32),
        pltpu.VMEM((SIDE, SIDE, CP), F32),
        pltpu.VMEM((SIDE, SIDE, CP), F32),
        pltpu.VMEM((NB, CELLS, HID), BF),
        pltpu.VMEM((NB, CELLS, HID), BF),
        pltpu.VMEM((NB, CELLS, C), F32),
        pltpu.VMEM((NB, CELLS, 1), F32),
        pltpu.VMEM((NB, CELLS, C), BF),
        pltpu.VMEM((49, 8, CP), F32),
        pltpu.VMEM((64, CP), F32),
        pltpu.VMEM((CELLS, C), F32),
    ]


def compute(h, image, cot, weights, small):
    vm = pl.BlockSpec(memory_space=pltpu.VMEM)
    return pl.pallas_call(
        compute_kernel,
        out_shape=jax.ShapeDtypeStruct((NB, ROWS, 128), BF),
        in_specs=[pl.BlockSpec(memory_space=pltpu.SMEM), vm, vm, vm, vm],
        out_specs=vm,
        scratch_shapes=compute_scratch(),
        compiler_params=pltpu.CompilerParams(vmem_limit_bytes=60 * 2**20),
        cost_estimate=pl.CostEstimate(flops=12 * 10**9, bytes_accessed=30 * 10**6, transcendentals=3 * 10**6),
    )(h, image, cot, weights, small)


def pack_small(dw_kernel, dw_bias, gain, nbias, up_bias, down_bias, scale):
    n = dw_kernel.shape[0]
    rows = jnp.concatenate([dw_kernel.reshape(n, 49, C), dw_bias[:, None], gain[:, None], nbias[:, None], down_bias[:, None], scale[:, None]], axis=1)
    rows = jnp.pad(rows, ((0, 0), (0, 0), (0, CP - C)))
    up = jnp.pad(up_bias, ((0, 0), (0, 4 * CP - HID))).reshape(n, 4, CP)
    return jnp.concatenate([rows, up, jnp.zeros((n, 6, CP), F32)], axis=1)


HALF, QUART, PIECE = ROWS // 2, ROWS // 8, ROWS // 32
MESH = pl.DeviceIdType.MESH


class Place:
    def __init__(self):
        s, d = lax.axis_index("section"), lax.axis_index("dp")
        self.s, self.d = s, d
        self.core = d % 2
        self.z = (d // 32) * 4 + s
        self.step1 = 2 + 6 * self.core
        self.step2 = 10 - self.step1
        self.f1 = (d // self.step1) % 4
        self.f2 = (d // self.step2) % 4
        self.half = pl.multiple_of(self.core * HALF, HALF)

    def sibling(self):
        return (self.s, self.d + 1 - 2 * self.core)

    def first(self, k):
        q = (self.f1 + k) % 4
        return q, (self.s, self.d + (q - self.f1) * self.step1)

    def second(self, k):
        q = (self.f2 + k) % 4
        return q, (self.s, self.d + (q - self.f2) * self.step2)

    def up_z(self, k):
        z = (self.z + k) % 8
        return (z % 4, (z // 4) * 32 + self.d % 32)


def greet(devices):
    barrier = pltpu.get_barrier_semaphore()
    for device in devices:
        pl.semaphore_signal(barrier, inc=1, device_id=device, device_id_type=MESH)
    pl.semaphore_wait(barrier, len(devices))


def remote(src, dst, send, recv, device):
    return pltpu.make_async_remote_copy(src_ref=src, dst_ref=dst, send_sem=send, recv_sem=recv, device_id=device, device_id_type=MESH)


def add_into(dst_ref, b, base, count, src_refs):
    def step(i, _):
        rows = pl.ds(pl.multiple_of(base + i * PIECE, 16), PIECE)
        own = pl.ds(pl.multiple_of(i * PIECE, 16), PIECE)
        total = dst_ref[b, rows, :].astype(F32)
        for src in src_refs:
            total = total + src[own, :].astype(F32)
        dst_ref[b, rows, :] = total.astype(BF)
        return 0

    lax.fori_loop(0, count, step, 0)


class Reduce:
    def __init__(self, at, g_ref, fin_ref, cr, xr, yr, zr, sems):
        self.at, self.g, self.fin = at, g_ref, fin_ref
        self.cr, self.xr, self.yr, self.zr = cr, xr, yr, zr
        self.sems = sems

    def core_copy(self, b):
        at, (cs, crs) = self.at, self.sems[0]
        other = pl.multiple_of((1 - at.core) * HALF, HALF)
        return remote(self.g.at[b, pl.ds(other, HALF)], self.cr.at[b], cs.at[b], crs.at[b], at.sibling())

    def first_copy(self, b, k):
        at, (xs, xrs) = self.at, self.sems[1]
        q, device = at.first(k)
        rows = pl.ds(pl.multiple_of(at.half + q * QUART, 16), QUART)
        return remote(self.g.at[b, rows], self.xr.at[b, k - 1], xs.at[b, k - 1], xrs.at[b, k - 1], device)

    def second_copy(self, b, k):
        at, (ys, yrs) = self.at, self.sems[2]
        q, device = at.second(k)
        rows = pl.ds(pl.multiple_of(at.half + at.f1 * QUART + q * PIECE, 16), PIECE)
        return remote(self.g.at[b, rows], self.yr.at[b, k - 1], ys.at[b, k - 1], yrs.at[b, k - 1], device)

    def piece(self):
        at = self.at
        return pl.multiple_of(at.half + at.f1 * QUART + at.f2 * PIECE, 16)

    def z_copy(self, b, hi, source):
        at, (zs, zrs) = self.at, self.sems[3]
        device = (b % 4, hi * 32 + at.d % 32)
        return remote(self.g.at[b, pl.ds(self.piece(), PIECE)], self.zr.at[b // 4, source], zs.at[b, hi], zrs.at[b // 4, source], device)

    def back_second(self, l, k):
        at, (s, r) = self.at, self.sems[4]
        _, device = at.second(k)
        rows = pl.ds(self.piece(), PIECE)
        return remote(self.fin.at[l, rows], self.fin.at[l, rows], s.at[l, k - 1], r.at[l, k - 1], device)

    def back_second_in(self, l, k):
        at, (s, r) = self.at, self.sems[4]
        q, device = at.second(4 - k)
        rows = pl.ds(pl.multiple_of(at.half + at.f1 * QUART + q * PIECE, 16), PIECE)
        return remote(self.fin.at[l, rows], self.fin.at[l, rows], s.at[l, k - 1], r.at[l, k - 1], device)

    def back_first(self, l, k):
        at, (s, r) = self.at, self.sems[5]
        _, device = at.first(k)
        rows = pl.ds(pl.multiple_of(at.half + at.f1 * QUART, 16), QUART)
        return remote(self.fin.at[l, rows], self.fin.at[l, rows], s.at[l, k - 1], r.at[l, k - 1], device)

    def back_first_in(self, l, k):
        at, (s, r) = self.at, self.sems[5]
        q, device = at.first(4 - k)
        rows = pl.ds(pl.multiple_of(at.half + q * QUART, 16), QUART)
        return remote(self.fin.at[l, rows], self.fin.at[l, rows], s.at[l, k - 1], r.at[l, k - 1], device)

    def back_core(self, l, core):
        at, (s, r) = self.at, self.sems[6]
        rows = pl.ds(pl.multiple_of(core * HALF, HALF), HALF)
        return remote(self.fin.at[l, rows], self.fin.at[l, rows], s.at[l], r.at[l], at.sibling())

    def stage0(self, b):
        self.core_copy(b).start()

    def stage1(self, b):
        self.core_copy(b).wait()
        add_into(self.g, b, self.at.half, 16, [self.cr.at[b]])
        for k in (2, 1, 3):
            self.first_copy(b, k).start()

    def stage2(self, b):
        for k in (1, 2, 3):
            self.first_copy(b, k).wait()
        add_into(self.g, b, self.at.half + self.at.f1 * QUART, 4, [self.xr.at[b, k] for k in range(3)])
        for k in (2, 1, 3):
            self.second_copy(b, k).start()

    def stage3(self, b):
        at = self.at
        for k in (1, 2, 3):
            self.second_copy(b, k).wait()
        add_into(self.g, b, self.piece(), 1, [self.yr.at[b, k] for k in range(3)])
        for hi in range(2):
            @pl.when(at.z != hi * 4 + b % 4)
            def _():
                self.z_copy(b, hi, at.z).start()

    def stage4(self, b):
        at = self.at
        for hi in range(2):
            @pl.when(at.z != hi * 4 + b % 4)
            def _():
                self.z_copy(b, hi, at.z).wait_send()

        @pl.when(at.s == b % 4)
        def _():
            l = b // 4
            for k in range(1, 8):
                self.z_copy(b, 0, (at.z + k) % 8).wait_recv()
            rows = pl.ds(self.piece(), PIECE)
            self.zr[l, at.z] = self.g[b, rows, :]
            total = self.zr[l, 0].astype(F32)
            for z in range(1, 8):
                total = total + self.zr[l, z].astype(F32)
            self.fin[l, rows, :] = total.astype(BF)
            for k in (2, 1, 3):
                self.back_second(l, k).start()

    def stage5(self, b):
        at = self.at

        @pl.when(at.s == b % 4)
        def _():
            l = b // 4
            for k in (1, 2, 3):
                self.back_second(l, k).wait_send()
                self.back_second_in(l, k).wait_recv()
            for k in (2, 1, 3):
                self.back_first(l, k).start()

    def stage6(self, b):
        at = self.at

        @pl.when(at.s == b % 4)
        def _():
            l = b // 4
            for k in (1, 2, 3):
                self.back_first(l, k).wait_send()
                self.back_first_in(l, k).wait_recv()
            self.back_core(l, at.core).start()

    def stage7(self, b):
        at = self.at

        @pl.when(at.s == b % 4)
        def _():
            l = b // 4
            self.back_core(l, at.core).wait_send()
            self.back_core(l, 1 - at.core).wait_recv()

    def stages(self):
        return [self.stage0, self.stage1, self.stage2, self.stage3, self.stage4, self.stage5, self.stage6, self.stage7]


def reduce_partners(at):
    return [at.sibling()] + [at.first(k)[1] for k in (1, 2, 3)] + [at.second(k)[1] for k in (1, 2, 3)] + [at.up_z(k) for k in range(1, 8)]


def pair(*shape):
    return [pltpu.SemaphoreType.DMA(shape), pltpu.SemaphoreType.DMA(shape)]


def reduce_scratch():
    buffers = [
        pltpu.VMEM((NB, HALF, 128), BF),
        pltpu.VMEM((NB, 3, QUART, 128), BF),
        pltpu.VMEM((NB, 3, PIECE, 128), BF),
        pltpu.VMEM((2, 8, PIECE, 128), BF),
    ]
    sems = pair(NB) + pair(NB, 3) + pair(NB, 3)
    sems += [pltpu.SemaphoreType.DMA((NB, 2)), pltpu.SemaphoreType.DMA((2, 8))]
    sems += pair(2, 3) + pair(2, 3) + pair(2)
    return buffers + sems


def make_reduce(at, g_ref, fin_ref, refs):
    sems = [tuple(refs[4 + 2 * i : 6 + 2 * i]) for i in range(7)]
    return Reduce(at, g_ref, fin_ref, *refs[:4], sems)


def reduce_kernel(g_in, fin_ref, g_ref, copy_sem, *refs):
    at = Place()
    red = make_reduce(at, g_ref, fin_ref, refs)
    load = pltpu.make_async_copy(g_in, g_ref, copy_sem)
    load.start()
    greet(reduce_partners(at))
    load.wait()
    stages = red.stages()

    def tick(t, _):
        for n, stage in enumerate(stages):
            b = NB - 1 - (t - n)

            @pl.when((b >= 0) & (b < NB))
            def _():
                stage(b)
        return 0

    lax.fori_loop(0, NB + len(stages) - 1, tick, 0)


def reduce_grads(g):
    return pl.pallas_call(
        reduce_kernel,
        out_shape=jax.ShapeDtypeStruct((2, ROWS, 128), BF),
        in_specs=[pl.BlockSpec(memory_space=pl.ANY)],
        out_specs=pl.BlockSpec(memory_space=pltpu.VMEM),
        scratch_shapes=[pltpu.VMEM((NB, ROWS, 128), BF), pltpu.SemaphoreType.DMA] + reduce_scratch(),
        compiler_params=pltpu.CompilerParams(collective_id=1, has_side_effects=True, vmem_limit_bytes=60 * 2**20),
        cost_estimate=pl.CostEstimate(flops=10**7, bytes_accessed=30 * 10**6, transcendentals=0),
    )(g)


class Gather:
    def __init__(self, at, w_ref, small_ref, sems):
        self.at, self.w, self.small = at, w_ref, small_ref
        self.wz, self.sz, self.wc, self.sc = sems

    def rows(self, core, n):
        return pl.ds(pl.multiple_of(core * n, n), n)

    def copies(self, l, section, kind, device):
        at, b = self.at, l * 4 + section % 4
        w = self.w.at[b, self.rows(at.core, C)]
        small = self.small.at[b, self.rows(at.core, 32)]
        return [
            remote(w, w, self.wz[0].at[l, kind], self.wz[1].at[l, kind], device),
            remote(small, small, self.sz[0].at[l, kind], self.sz[1].at[l, kind], device),
        ]

    def across(self, l, section, kind, core):
        at, b = self.at, l * 4 + section % 4
        w = self.w.at[b, self.rows(core, C)]
        small = self.small.at[b, self.rows(core, 32)]
        return [
            remote(w, w, self.wc[0].at[l, kind], self.wc[1].at[l, kind], at.sibling()),
            remote(small, small, self.sc[0].at[l, kind], self.sc[1].at[l, kind], at.sibling()),
        ]

    def begin(self, l):
        at = self.at
        for kind, k in ((0, 1), (1, -1)):
            for c in self.copies(l, at.s, kind, at.up_z(k)):
                c.start()

    def pass_on(self, l):
        at = self.at
        for kind, k in ((0, -1), (1, 1)):
            for c in self.copies(l, at.s + 4 + k, kind, at.up_z(k)):
                c.wait_recv()
            onward = at.core == 1 - kind

            @pl.when(onward)
            def _():
                for c in self.copies(l, at.s + 4 + k, 2, at.up_z(-k)):
                    c.start()
            for c in self.across(l, at.s + 4 + k, kind, at.core):
                c.start()

    def finish(self, l):
        at = self.at
        far = at.up_z(1)
        for c in self.copies(l, at.s + 2, 2, far):
            c.wait_recv()
        for c in self.across(l, at.s + 2, 2, at.core):
            c.start()
        for kind, k in ((0, -1), (1, 1), (2, 2)):
            for c in self.across(l, at.s + 4 + k, kind, 1 - at.core):
                c.wait_recv()

    def drain(self, l):
        at = self.at
        for kind in range(3):
            for c in self.copies(l, at.s, kind, at.up_z(1)):
                c.wait_send()
            for c in self.across(l, at.s, kind, at.core):
                c.wait_send()


def gather_partners(at):
    return [at.sibling(), at.up_z(1), at.up_z(-1)]


def gather_scratch():
    return pair(2, 3) + pair(2, 3) + pair(2, 3) + pair(2, 3)


def make_gather(at, w_ref, small_ref, sems):
    return Gather(at, w_ref, small_ref, [tuple(sems[2 * i : 2 * i + 2]) for i in range(4)])


def gather_kernel(w_in, small_in, w_ref, small_ref, own_sem, *sems):
    at = Place()
    own = []
    for l in range(2):
        own.append(pltpu.make_async_copy(w_in.at[l], w_ref.at[l * 4 + at.s], own_sem.at[l, 0]))
        own.append(pltpu.make_async_copy(small_in.at[l], small_ref.at[l * 4 + at.s], own_sem.at[l, 1]))
    for c in own:
        c.start()
    greet(gather_partners(at))
    for c in own:
        c.wait()
    gather = make_gather(at, w_ref, small_ref, sems)
    for l in range(2):
        gather.begin(l)
    for l in range(2):
        gather.pass_on(l)
        gather.finish(l)
    for l in range(2):
        gather.drain(l)


def gather_weights(w, small):
    anyw = pl.BlockSpec(memory_space=pl.ANY)
    vm = pl.BlockSpec(memory_space=pltpu.VMEM)
    return pl.pallas_call(
        gather_kernel,
        out_shape=(jax.ShapeDtypeStruct((NB, 2 * C, HID), BF), jax.ShapeDtypeStruct((NB, 64, CP), F32)),
        in_specs=[anyw, anyw],
        out_specs=(vm, vm),
        scratch_shapes=[pltpu.SemaphoreType.DMA((2, 2))] + gather_scratch(),
        compiler_params=pltpu.CompilerParams(collective_id=0, has_side_effects=True, vmem_limit_bytes=60 * 2**20),
        cost_estimate=pl.CostEstimate(flops=10**6, bytes_accessed=30 * 10**6, transcendentals=0),
    )(w, small)


def unpack(fin):
    up = fin[:, :3200].reshape(2, 10, C, 128).transpose(0, 2, 1, 3).reshape(2, C, HID)
    down = fin[:, 3200:6400].reshape(2, 10, C, 128).transpose(0, 1, 3, 2).reshape(2, HID, C)
    small = fin[:, 6400:6592].astype(F32).reshape(2, 3, 64, 128).transpose(0, 2, 1, 3).reshape(2, 64, CP)
    up_bias = small[:, 54:58].reshape(2, 4 * CP)[:, :HID]
    row = lambda i: small[:, i, :C]
    parts = (small[:, :49, :C].reshape(2, 7, 7, C), row(49), row(50), row(51), up, up_bias, down, row(52), row(53))
    return tuple(p[:, None] for p in parts)


def body(images, cotangent, heights, dw_kernel, dw_bias, norm_gain, norm_bias, up_weight, up_bias, down_weight, down_bias, layer_scale):
    s = lax.axis_index("section")
    pick = lambda a: lax.dynamic_index_in_dim(a[:, 0], s, 0, keepdims=False).reshape(CELLS, C)
    w = jnp.concatenate([up_weight[:, 0], down_weight[:, 0].swapaxes(1, 2)], axis=1)
    small = pack_small(*(a[:, 0] for a in (dw_kernel, dw_bias, norm_gain, norm_bias, up_bias, down_bias, layer_scale)))
    height = lax.dynamic_slice_in_dim(heights, s, 1)
    w_all, small_all = gather_weights(w, small)
    grads = compute(height, pick(images), pick(cotangent), w_all, small_all)
    return unpack(reduce_grads(grads))


def solution(mesh):
    three, two = P(None, "section", None, None), P(None, "section", None)
    five = P(None, "section", None, None, None)
    image = P(None, "dp", None, None, None)
    weights = (five, two, two, two, three, two, three, two, two)
    return jax.shard_map(body, mesh=mesh, in_specs=(image, image, P()) + weights, out_specs=weights, check_vma=False)
```

```python
import jax
import jax.numpy as jnp
from jax import lax
from jax.experimental import pallas as pl
from jax.experimental.pallas import tpu as pltpu
from jax.sharding import PartitionSpec as P

C, HID, SIDE, NB = 320, 1280, 16, 8
CP = 384
CELLS = SIDE * SIDE
ROWS = 6656
BF, F32 = jnp.bfloat16, jnp.float32
K0, K1 = 0.7978845608028654, 0.044715
T_LANES = (((1,), (1,)), ((), ()))
T_ROWS = (((0,), (0,)), ((), ()))


def dot(a, b, dims=(((1,), (0,)), ((), ()))):
    return lax.dot_general(a, b, dims, preferred_element_type=F32)


def lane_tile(t):
    return pl.ds(pl.multiple_of(t * 128, 128), 128)


def shift_columns(pad_ref, shift_ref, first, step):
    for dj in range(7):
        at = first + step * dj
        shift_ref[dj] = pad_ref[:, at : at + SIDE, :]


def taps_of(small_ref, b, dj, lanes):
    return [jnp.broadcast_to(small_ref[b, dr * 7 + dj : dr * 7 + dj + 1, lanes], (8, 128)) for dr in range(7)]


def conv_forward(shift_ref, small_ref, b, out_ref):
    def tile(t, _):
        lanes = lane_tile(t)
        for half in range(2):
            cols = pl.ds(8 * half, 8)
            acc = [jnp.broadcast_to(small_ref[b, 49:50, lanes], (8, 128))] * SIDE
            for dj in range(7):
                taps = taps_of(small_ref, b, dj, lanes)
                for r in range(SIDE):
                    x = shift_ref[dj, r, cols, lanes]
                    for dr in range(7):
                        i = r - dr + 3
                        if 0 <= i < SIDE:
                            acc[i] = acc[i] + x * taps[dr]
            for i in range(SIDE):
                out_ref[i, cols, lanes] = acc[i]
        return 0

    lax.fori_loop(0, 3, tile, 0)


def conv_backward(shift_ref, x_ref, small_ref, b, dx_ref, dk_ref):
    def tile(t, _):
        lanes = lane_tile(t)
        for half in range(2):
            cols = pl.ds(8 * half, 8)
            xs = [x_ref[i, cols, lanes] for i in range(SIDE)]
            acc = [None] * SIDE
            for dj in range(7):
                taps = taps_of(small_ref, b, dj, lanes)
                dks = [None] * 7
                for r in range(SIDE):
                    g = shift_ref[dj, r, cols, lanes]
                    for dr in range(7):
                        i = r + dr - 3
                        if 0 <= i < SIDE:
                            p = g * taps[dr]
                            acc[i] = p if acc[i] is None else acc[i] + p
                            p = g * xs[i]
                            dks[dr] = p if dks[dr] is None else dks[dr] + p
                for dr in range(7):
                    if half == 0:
                        dk_ref[dr * 7 + dj, :, lanes] = dks[dr]
                    else:
                        dk_ref[dr * 7 + dj, :, lanes] += dks[dr]
            for i in range(SIDE):
                dx_ref[i, cols, lanes] = acc[i]
        return 0

    lax.fori_loop(0, 3, tile, 0)


def weight_chunk(w_ref, b, base, n):
    at = base + 640 * n
    return jnp.concatenate([w_ref[b, at : at + C, :], w_ref[b, at + C : at + 2 * C, :]], axis=1)


def small_row(small_ref, b, row):
    return small_ref[b, row : row + 1, 0:C]


def up_bias_chunk(small_ref, b, n):
    parts = []
    for t in (2 * n, 2 * n + 1):
        parts.append(small_ref[b, 54 + t // 3 : 55 + t // 3, (t % 3) * 128 : (t % 3 + 1) * 128])
    return jnp.concatenate(parts, axis=1)


def window_of(h):
    cell = lax.broadcasted_iota(jnp.int32, (CELLS, 1), 0)
    return ((cell // SIDE < h) & (cell % SIDE < h)).astype(F32)


def block_forward(b, h, w_ref, small_ref, v_ref, pad_ref, shift_ref, mix_ref, act_ref, slope_ref, xhat_ref, inv_ref, proj_ref):
    v = v_ref[b].astype(F32)
    pad_ref[:, 8:24, 0:C] = v.reshape(SIDE, SIDE, C)
    shift_columns(pad_ref, shift_ref, 5, 1)
    conv_forward(shift_ref, small_ref, b, mix_ref)
    mixed = mix_ref[:, :, 0:C].reshape(CELLS, C)
    center = jnp.sum(mixed, axis=1, keepdims=True) * (1.0 / C)
    mixed = mixed - center
    inv = lax.rsqrt(jnp.sum(mixed * mixed, axis=1, keepdims=True) * (1.0 / C) + 1e-6)
    xhat = mixed * inv
    xhat_ref[b] = xhat
    inv_ref[b] = inv
    normed = (xhat * small_row(small_ref, b, 50) + small_row(small_ref, b, 51)).astype(BF)
    proj = jnp.broadcast_to(small_row(small_ref, b, 52), (CELLS, C))
    for n in range(5):
        cols = slice(256 * n, 256 * n + 256)
        u = dot(normed, weight_chunk(w_ref, b, 0, n)) + up_bias_chunk(small_ref, b, n)
        uu = u * u
        t = jnp.tanh(u * (K0 + (K0 * K1) * uu))
        lift = 0.5 + 0.5 * t
        act = (u * lift).astype(BF)
        slope = lift + (u * (0.5 - 0.5 * t * t)) * (K0 + (3 * K0 * K1) * uu)
        act_ref[b, :, cols] = act
        slope_ref[b, :, cols] = slope.astype(BF)
        proj = proj + dot(act, weight_chunk(w_ref, b, 3200, n), T_LANES)
    proj_ref[b] = proj.astype(BF)
    out = (v + small_row(small_ref, b, 53) * proj) * window_of(h)
    return out.astype(BF)


def block_backward(b, h, g, w_ref, small_ref, v_ref, pad_ref, shift_ref, mix_ref, x_ref, act_ref, slope_ref, xhat_ref, inv_ref, proj_ref, dk_ref, sg_ref):
    g = g * window_of(h)
    sg_ref[53:54, 0:C] = jnp.sum(g * proj_ref[b].astype(F32), axis=0, keepdims=True)
    dproj = g * small_row(small_ref, b, 53)
    sg_ref[52:53, 0:C] = jnp.sum(dproj, axis=0, keepdims=True)
    dproj = dproj.astype(BF)
    xhat = xhat_ref[b]
    gain = small_row(small_ref, b, 50)
    normed = (xhat * gain + small_row(small_ref, b, 51)).astype(BF)
    dnormed = None
    for n in range(5):
        cols = slice(256 * n, 256 * n + 256)
        dact = dot(dproj, weight_chunk(w_ref, b, 3200, n))
        dhid = dact * slope_ref[b, :, cols].astype(F32)
        bias = jnp.sum(dhid, axis=0, keepdims=True)
        dhid = dhid.astype(BF)
        part = dot(dhid, weight_chunk(w_ref, b, 0, n), T_LANES)
        dnormed = part if dnormed is None else dnormed + part
        dup = dot(normed, dhid, T_ROWS).astype(BF)
        ddown = dot(dproj, act_ref[b, :, cols], T_ROWS).astype(BF)
        for k in range(2):
            t = 2 * n + k
            lanes = slice(128 * k, 128 * k + 128)
            w_ref[b, 320 * t : 320 * t + 320, :] = dup[:, lanes]
            w_ref[b, 3200 + 320 * t : 3520 + 320 * t, :] = ddown[:, lanes]
            sg_ref[54 + t // 3 : 55 + t // 3, (t % 3) * 128 : (t % 3 + 1) * 128] = bias[:, lanes]
    sg_ref[50:51, 0:C] = jnp.sum(dnormed * xhat, axis=0, keepdims=True)
    sg_ref[51:52, 0:C] = jnp.sum(dnormed, axis=0, keepdims=True)
    dxhat = dnormed * gain
    m0 = jnp.sum(dxhat, axis=1, keepdims=True) * (1.0 / C)
    m1 = jnp.sum(dxhat * xhat, axis=1, keepdims=True) * (1.0 / C)
    dmixed = inv_ref[b] * (dxhat - m0 - xhat * m1)
    sg_ref[49:50, 0:C] = jnp.sum(dmixed, axis=0, keepdims=True)
    pad_ref[:, 8:24, 0:C] = dmixed.reshape(SIDE, SIDE, C)
    x_ref[:, :, 0:C] = v_ref[b].astype(F32).reshape(SIDE, SIDE, C)
    shift_columns(pad_ref, shift_ref, 11, -1)
    conv_backward(shift_ref, x_ref, small_ref, b, mix_ref, dk_ref)
    sg_ref[0:49, :] = jnp.sum(dk_ref[...], axis=1)
    for j in range(3):
        w_ref[b, 6400 + 64 * j : 6464 + 64 * j, :] = sg_ref[:, 128 * j : 128 * j + 128].astype(BF)
    return (g + mix_ref[:, :, 0:C].reshape(CELLS, C)).astype(BF).astype(F32)


def clear(ref):
    ref[...] = jnp.zeros(ref.shape, ref.dtype)


def pack_small(dw_kernel, dw_bias, gain, nbias, up_bias, down_bias, scale):
    n = dw_kernel.shape[0]
    rows = jnp.concatenate([dw_kernel.reshape(n, 49, C), dw_bias[:, None], gain[:, None], nbias[:, None], down_bias[:, None], scale[:, None]], axis=1)
    rows = jnp.pad(rows, ((0, 0), (0, 0), (0, CP - C)))
    up = jnp.pad(up_bias, ((0, 0), (0, 4 * CP - HID))).reshape(n, 4, CP)
    return jnp.concatenate([rows, up, jnp.zeros((n, 6, CP), F32)], axis=1)


HALF, QUART, PIECE = ROWS // 2, ROWS // 8, ROWS // 32
MESH = pl.DeviceIdType.MESH


class Place:
    def __init__(self):
        s, d = lax.axis_index("section"), lax.axis_index("dp")
        self.s, self.d = s, d
        self.core = d % 2
        self.z = (d // 32) * 4 + s
        self.step1 = 2 + 6 * self.core
        self.step2 = 10 - self.step1
        self.f1 = (d // self.step1) % 4
        self.f2 = (d // self.step2) % 4
        self.half = pl.multiple_of(self.core * HALF, HALF)
        self.x, self.y = (d // 2) % 4, (d // 8) % 4
        self.color = (self.x + self.y) % 2

    def sibling(self):
        return (self.s, self.d + 1 - 2 * self.core)

    def first(self, k):
        q = (self.f1 + k) % 4
        return q, (self.s, self.d + (q - self.f1) * self.step1)

    def second(self, k):
        q = (self.f2 + k) % 4
        return q, (self.s, self.d + (q - self.f2) * self.step2)

    def beside(self, side):
        step, at = (2, self.x) if side < 2 else (8, self.y)
        k = 1 if side % 2 == 0 else 3
        return (self.s, self.d + ((at + k) % 4 - at) * step)

    def up_z(self, k):
        z = (self.z + k) % 8
        return (z % 4, (z // 4) * 32 + self.d % 32)


def greet(devices):
    barrier = pltpu.get_barrier_semaphore()
    for device in devices:
        pl.semaphore_signal(barrier, inc=1, device_id=device, device_id_type=MESH)
    pl.semaphore_wait(barrier, len(devices))


def remote(src, dst, send, recv, device):
    return pltpu.make_async_remote_copy(src_ref=src, dst_ref=dst, send_sem=send, recv_sem=recv, device_id=device, device_id_type=MESH)


def add_into(dst_ref, b, base, count, src_refs):
    def step(i, _):
        rows = pl.ds(pl.multiple_of(base + i * PIECE, 16), PIECE)
        own = pl.ds(pl.multiple_of(i * PIECE, 16), PIECE)
        total = dst_ref[b, rows, :].astype(F32)
        for src in src_refs:
            total = total + src[own, :].astype(F32)
        dst_ref[b, rows, :] = total.astype(BF)
        return 0

    lax.fori_loop(0, count, step, 0)


class Reduce:
    def __init__(self, at, g_ref, outs, fin_ref, cr, xr, yr, zr, sems):
        self.at, self.g, self.fin = at, g_ref, fin_ref
        self.up, self.down, self.small = outs
        self.cr, self.xr, self.yr, self.zr = cr, xr, yr, zr
        self.sems = sems

    def core_copy(self, b):
        at, (cs, crs) = self.at, self.sems[0]
        other = pl.multiple_of((1 - at.core) * HALF, HALF)
        return remote(self.g.at[b, pl.ds(other, HALF)], self.cr.at[b], cs.at[b], crs.at[b], at.sibling())

    def first_copy(self, b, k):
        at, (xs, xrs) = self.at, self.sems[1]
        q, device = at.first(k)
        rows = pl.ds(pl.multiple_of(at.half + q * QUART, 16), QUART)
        return remote(self.g.at[b, rows], self.xr.at[b, k - 1], xs.at[b, k - 1], xrs.at[b, k - 1], device)

    def second_copy(self, b, k):
        at, (ys, yrs) = self.at, self.sems[2]
        q, device = at.second(k)
        rows = pl.ds(pl.multiple_of(at.half + at.f1 * QUART + q * PIECE, 16), PIECE)
        return remote(self.g.at[b, rows], self.yr.at[b, k - 1], ys.at[b, k - 1], yrs.at[b, k - 1], device)

    def piece(self):
        at = self.at
        return pl.multiple_of(at.half + at.f1 * QUART + at.f2 * PIECE, 16)

    def z_copy(self, b, hi, source):
        at, (zs, zrs) = self.at, self.sems[3]
        device = (b % 4, hi * 32 + at.d % 32)
        return remote(self.g.at[b, pl.ds(self.piece(), PIECE)], self.zr.at[b // 4, source], zs.at[b, hi], zrs.at[b // 4, source], device)

    def back_second(self, l, k):
        at, (s, r) = self.at, self.sems[4]
        _, device = at.second(k)
        rows = pl.ds(self.piece(), PIECE)
        return remote(self.fin.at[l, rows], self.fin.at[l, rows], s.at[l, k - 1], r.at[l, k - 1], device)

    def back_second_in(self, l, k):
        at, (s, r) = self.at, self.sems[4]
        q, device = at.second(4 - k)
        rows = pl.ds(pl.multiple_of(at.half + at.f1 * QUART + q * PIECE, 16), PIECE)
        return remote(self.fin.at[l, rows], self.fin.at[l, rows], s.at[l, k - 1], r.at[l, k - 1], device)

    def back_first(self, l, k):
        at, (s, r) = self.at, self.sems[5]
        _, device = at.first(k)
        rows = pl.ds(pl.multiple_of(at.half + at.f1 * QUART, 16), QUART)
        return remote(self.fin.at[l, rows], self.fin.at[l, rows], s.at[l, k - 1], r.at[l, k - 1], device)

    def back_first_in(self, l, k):
        at, (s, r) = self.at, self.sems[5]
        q, device = at.first(4 - k)
        rows = pl.ds(pl.multiple_of(at.half + q * QUART, 16), QUART)
        return remote(self.fin.at[l, rows], self.fin.at[l, rows], s.at[l, k - 1], r.at[l, k - 1], device)

    def back_core(self, l, core):
        at, (s, r) = self.at, self.sems[6]
        rows = pl.ds(pl.multiple_of(core * HALF, HALF), HALF)
        return remote(self.fin.at[l, rows], self.fin.at[l, rows], s.at[l], r.at[l], at.sibling())

    def stage0(self, b):
        self.core_copy(b).start()

    def stage1(self, b):
        self.core_copy(b).wait()
        add_into(self.g, b, self.at.half, 16, [self.cr.at[b]])
        for k in (2, 1, 3):
            self.first_copy(b, k).start()

    def stage2(self, b):
        for k in (1, 2, 3):
            self.first_copy(b, k).wait()
        add_into(self.g, b, self.at.half + self.at.f1 * QUART, 4, [self.xr.at[b, k] for k in range(3)])
        for k in (2, 1, 3):
            self.second_copy(b, k).start()

    def stage3(self, b):
        at = self.at
        for k in (1, 2, 3):
            self.second_copy(b, k).wait()
        add_into(self.g, b, self.piece(), 1, [self.yr.at[b, k] for k in range(3)])
        for hi in range(2):
            @pl.when(at.z != hi * 4 + b % 4)
            def _():
                self.z_copy(b, hi, at.z).start()

    def stage4(self, b):
        at = self.at
        for hi in range(2):
            @pl.when(at.z != hi * 4 + b % 4)
            def _():
                self.z_copy(b, hi, at.z).wait_send()

        @pl.when(at.s == b % 4)
        def _():
            l = b // 4
            for k in range(1, 8):
                self.z_copy(b, 0, (at.z + k) % 8).wait_recv()
            rows = pl.ds(self.piece(), PIECE)
            self.zr[l, at.z] = self.g[b, rows, :]
            total = self.zr[l, 0].astype(F32)
            for z in range(1, 8):
                total = total + self.zr[l, z].astype(F32)
            self.fin[l, rows, :] = total.astype(BF)
            for k in (2, 1, 3):
                self.back_second(l, k).start()

    def stage5(self, b):
        at = self.at

        @pl.when(at.s == b % 4)
        def _():
            l = b // 4
            for k in (1, 2, 3):
                self.back_second(l, k).wait_send()
                self.back_second_in(l, k).wait_recv()
            for k in (2, 1, 3):
                self.back_first(l, k).start()

    def stage6(self, b):
        at = self.at

        @pl.when(at.s == b % 4)
        def _():
            l = b // 4
            for k in (1, 2, 3):
                self.back_first(l, k).wait_send()
                self.back_first_in(l, k).wait_recv()
            self.back_core(l, at.core).start()

    def stage7(self, b):
        at = self.at

        @pl.when(at.s == b % 4)
        def _():
            l = b // 4
            self.back_core(l, at.core).wait_send()
            self.back_core(l, 1 - at.core).wait_recv()
            for t in range(10):
                lanes = slice(128 * t, 128 * t + 128)
                self.up[l, :, lanes] = self.fin[l, C * t : C * t + C, :]
                self.down[l, :, lanes] = self.fin[l, 3200 + C * t : 3200 + C * t + C, :]
            for t in range(3):
                self.small[l, :, 128 * t : 128 * t + 128] = self.fin[l, 6400 + 64 * t : 6464 + 64 * t, :].astype(F32)

    def stages(self):
        return [self.stage0, self.stage1, self.stage2, self.stage3, self.stage4, self.stage5, self.stage6, self.stage7]


def reduce_partners(at):
    return [at.sibling()] + [at.first(k)[1] for k in (1, 2, 3)] + [at.second(k)[1] for k in (1, 2, 3)] + [at.up_z(k) for k in range(1, 8)]


def pair(*shape):
    return [pltpu.SemaphoreType.DMA(shape), pltpu.SemaphoreType.DMA(shape)]


def reduce_scratch():
    buffers = [
        pltpu.VMEM((2, ROWS, 128), BF),
        pltpu.VMEM((NB, HALF, 128), BF),
        pltpu.VMEM((NB, 3, QUART, 128), BF),
        pltpu.VMEM((NB, 3, PIECE, 128), BF),
        pltpu.VMEM((2, 8, PIECE, 128), BF),
    ]
    sems = pair(NB) + pair(NB, 3) + pair(NB, 3)
    sems += [pltpu.SemaphoreType.DMA((NB, 2)), pltpu.SemaphoreType.DMA((2, 8))]
    sems += pair(2, 3) + pair(2, 3) + pair(2)
    return buffers + sems


def make_reduce(at, g_ref, outs, refs):
    sems = [tuple(refs[5 + 2 * i : 7 + 2 * i]) for i in range(7)]
    return Reduce(at, g_ref, outs, *refs[:5], sems)


WHALF, SHARE, PART = 3200, 1600, 400


class Gather:
    def __init__(self, at, w_ref, small_ref, sems):
        self.at, self.w, self.small_ref = at, w_ref, small_ref
        self.zs, self.ps, self.cs, self.small_zs, self.small_cs = sems

    def block(self, l, kind):
        return l * 4 + (self.at.s + (3, 1, 2)[kind]) % 4

    def share(self, core, color):
        return pl.multiple_of(core * WHALF + color * SHARE, 16)

    def along_z(self, l, b, kind, device):
        at = self.at
        w = self.w.at[b, pl.ds(self.share(at.core, at.color), SHARE)]
        small = self.small_ref.at[b, pl.ds(pl.multiple_of(at.core * 32, 32), 32)]
        return [
            remote(w, w, self.zs[0].at[l, kind], self.zs[1].at[l, kind], device),
            remote(small, small, self.small_zs[0].at[l, kind], self.small_zs[1].at[l, kind], device),
        ]

    def in_plane(self, l, kind, side, color):
        at = self.at
        w = self.w.at[self.block(l, kind), pl.ds(pl.multiple_of(self.share(at.core, color) + side * PART, 16), PART)]
        return remote(w, w, self.ps[0].at[l, kind, side], self.ps[1].at[l, kind, side], at.beside(side))

    def to_sibling(self, l, kind, core, color, which):
        w = self.w.at[self.block(l, kind), pl.ds(self.share(core, color), SHARE)]
        return remote(w, w, self.cs[0].at[l, kind, which], self.cs[1].at[l, kind, which], self.at.sibling())

    def small_to_sibling(self, l, kind, core):
        small = self.small_ref.at[self.block(l, kind), pl.ds(pl.multiple_of(core * 32, 32), 32)]
        return remote(small, small, self.small_cs[0].at[l, kind], self.small_cs[1].at[l, kind], self.at.sibling())

    def begin(self, l):
        at = self.at
        for kind, k in ((0, 1), (1, -1)):
            for c in self.along_z(l, l * 4 + at.s, kind, at.up_z(k)):
                c.start()

    def spread(self, l, kind):
        at = self.at
        for side in range(4):
            self.in_plane(l, kind, side, at.color).start()
        self.to_sibling(l, kind, at.core, at.color, 0).start()
        self.small_to_sibling(l, kind, at.core).start()

    def near(self, l):
        at = self.at
        for kind, k in ((0, -1), (1, 1)):
            b = self.block(l, kind)
            for c in self.along_z(l, b, kind, at.up_z(k)):
                c.wait_recv()

            @pl.when(at.core == 1 - kind)
            def _():
                for c in self.along_z(l, b, 2, at.up_z(-k)):
                    c.start()
        for kind in range(2):
            self.spread(l, kind)

    def close_plane(self, l, kind):
        at = self.at
        for side in range(4):
            self.in_plane(l, kind, side, 1 - at.color).wait_recv()
        self.to_sibling(l, kind, at.core, 1 - at.color, 1).start()

    def far(self, l):
        at = self.at
        for c in self.along_z(l, self.block(l, 2), 2, at.up_z(1)):
            c.wait_recv()
        self.spread(l, 2)
        for kind in range(2):
            self.close_plane(l, kind)

    def last(self, l):
        at = self.at
        self.close_plane(l, 2)
        for kind in range(3):
            self.to_sibling(l, kind, 1 - at.core, at.color, 0).wait_recv()
            self.to_sibling(l, kind, 1 - at.core, 1 - at.color, 1).wait_recv()
            self.small_to_sibling(l, kind, 1 - at.core).wait_recv()

    def drain(self, l):
        at = self.at
        for kind in range(3):
            for c in self.along_z(l, self.block(l, kind), kind, at.up_z(1)):
                c.wait_send()
            for side in range(4):
                self.in_plane(l, kind, side, at.color).wait_send()
            self.to_sibling(l, kind, at.core, at.color, 0).wait_send()
            self.to_sibling(l, kind, at.core, 1 - at.color, 1).wait_send()
            self.small_to_sibling(l, kind, at.core).wait_send()


def gather_scratch():
    return pair(2, 3) + pair(2, 3, 4) + pair(2, 3, 2) + pair(2, 3) + pair(2, 3)


def make_gather(at, w_ref, small_ref, sems):
    return Gather(at, w_ref, small_ref, [tuple(sems[2 * i : 2 * i + 2]) for i in range(5)])


def clear(ref):
    ref[...] = jnp.zeros(ref.shape, ref.dtype)


def step_kernel(heights_ref, images_ref, cot_ref, up_in, down_in, small_in, up_out, down_out, small_out, w_ref, small_ref, image_ref, v_ref, pad_ref, shift_ref, mix_ref, x_ref, act_ref, slope_ref, xhat_ref, inv_ref, proj_ref, dk_ref, sg_ref, g_ref, load_sem, own_sem, *refs):
    at = Place()
    gather = make_gather(at, w_ref, small_ref, refs[:10])
    red = make_reduce(at, w_ref, (up_out, down_out, small_out), refs[10:])
    own = [[], []]
    for l in range(2):
        b = l * 4 + at.s
        for t in range(10):
            lanes = pl.ds(128 * t, 128)
            own[l].append(pltpu.make_async_copy(up_in.at[l, :, lanes], w_ref.at[b, pl.ds(C * t, C)], own_sem.at[l, t]))
            own[l].append(pltpu.make_async_copy(down_in.at[l, :, lanes], w_ref.at[b, pl.ds(3200 + C * t, C)], own_sem.at[l, 10 + t]))
        own[l].append(pltpu.make_async_copy(small_in.at[l], small_ref.at[b], own_sem.at[l, 20]))
    load = [pltpu.make_async_copy(images_ref.at[at.s, 0], image_ref.at[0], load_sem.at[0]), pltpu.make_async_copy(cot_ref.at[at.s, 0], image_ref.at[1], load_sem.at[1])]
    for c in own[0] + own[1] + load:
        c.start()
    greet([at.sibling()] + [at.first(k)[1] for k in (1, 2, 3)] + [at.second(k)[1] for k in (1, 2, 3)] + [at.up_z(k) for k in range(1, 8)])
    for c in own[0]:
        c.wait()
    gather.begin(0)
    clear(pad_ref)
    clear(x_ref)
    clear(sg_ref)
    h = heights_ref[at.s]
    for c in load + own[1]:
        c.wait()
    v_ref[0] = (image_ref[0].astype(F32).reshape(CELLS, C) * window_of(h)).astype(BF)
    gather.near(0)
    gather.begin(1)
    gather.far(0)
    gather.last(0)

    def forward(b, _):
        v_ref[b + 1] = block_forward(b, h, w_ref, small_ref, v_ref, pad_ref, shift_ref, mix_ref, act_ref, slope_ref, xhat_ref, inv_ref, proj_ref)
        for n, part in ((1, gather.near), (2, gather.far), (3, gather.last)):
            @pl.when(b == n)
            def _():
                part(1)
        return 0

    lax.fori_loop(0, NB, forward, 0)
    gather.drain(0)
    gather.drain(1)
    g_ref[...] = image_ref[1].astype(F32).reshape(CELLS, C)
    stages = red.stages()

    def tick(t, _):
        b = NB - 1 - t

        @pl.when(b >= 0)
        def _():
            w_ref[b, 6592:6656, :] = jnp.zeros((64, 128), BF)
            g_ref[...] = block_backward(b, h, g_ref[...], w_ref, small_ref, v_ref, pad_ref, shift_ref, mix_ref, x_ref, act_ref, slope_ref, xhat_ref, inv_ref, proj_ref, dk_ref, sg_ref)
        for n, stage in enumerate(stages):
            @pl.when((b + n >= 0) & (b + n < NB))
            def _():
                stage(b + n)
        return 0

    lax.fori_loop(0, NB + len(stages) - 1, tick, 0)


def step(heights, images, cotangent, up, down, small):
    hbm = pl.BlockSpec(memory_space=pl.ANY)
    vm = pl.BlockSpec(memory_space=pltpu.VMEM)
    scratch = [
        pltpu.VMEM((NB, ROWS, 128), BF),
        pltpu.VMEM((NB, 64, CP), F32),
        pltpu.VMEM((2, SIDE, SIDE, C), BF),
        pltpu.VMEM((NB + 1, CELLS, C), BF),
        pltpu.VMEM((SIDE, 32, CP), F32),
        pltpu.VMEM((7, SIDE, SIDE, CP), F32),
        pltpu.VMEM((SIDE, SIDE, CP), F32),
        pltpu.VMEM((SIDE, SIDE, CP), F32),
        pltpu.VMEM((NB, CELLS, HID), BF),
        pltpu.VMEM((NB, CELLS, HID), BF),
        pltpu.VMEM((NB, CELLS, C), F32),
        pltpu.VMEM((NB, CELLS, 1), F32),
        pltpu.VMEM((NB, CELLS, C), BF),
        pltpu.VMEM((49, 8, CP), F32),
        pltpu.VMEM((64, CP), F32),
        pltpu.VMEM((CELLS, C), F32),
        pltpu.SemaphoreType.DMA((2,)),
        pltpu.SemaphoreType.DMA((2, 21)),
    ]
    return pl.pallas_call(
        step_kernel,
        out_shape=(jax.ShapeDtypeStruct((2, C, HID), BF), jax.ShapeDtypeStruct((2, C, HID), BF), jax.ShapeDtypeStruct((2, 64, CP), F32)),
        in_specs=[pl.BlockSpec(memory_space=pltpu.SMEM)] + [hbm] * 5,
        out_specs=(vm, vm, vm),
        scratch_shapes=scratch + gather_scratch() + reduce_scratch(),
        compiler_params=pltpu.CompilerParams(collective_id=0, has_side_effects=True, vmem_limit_bytes=62 * 2**20),
        cost_estimate=pl.CostEstimate(flops=12 * 10**9, bytes_accessed=30 * 10**6, transcendentals=3 * 10**6),
    )(heights, images, cotangent, up, down, small)


def body(images, cotangent, heights, dw_kernel, dw_bias, norm_gain, norm_bias, up_weight, up_bias, down_weight, down_bias, layer_scale):
    small = pack_small(*(a[:, 0] for a in (dw_kernel, dw_bias, norm_gain, norm_bias, up_bias, down_bias, layer_scale)))
    up, down, small = step(heights, images, cotangent, up_weight[:, 0], down_weight[:, 0].swapaxes(1, 2), small)
    row = lambda i: small[:, i, :C]
    up_bias_grad = small[:, 54:58].reshape(2, 4 * CP)[:, :HID]
    parts = (small[:, :49, :C].reshape(2, 7, 7, C), row(49), row(50), row(51), up, up_bias_grad, down.swapaxes(1, 2), row(52), row(53))
    return tuple(p[:, None] for p in parts)


def solution(mesh):
    three, two = P(None, "section", None, None), P(None, "section", None)
    five = P(None, "section", None, None, None)
    image = P(None, "dp", None, None, None)
    weights = (five, two, two, two, three, two, three, two, two)
    return jax.shard_map(body, mesh=mesh, in_specs=(image, image, P()) + weights, out_specs=weights, check_vma=False)
```

```python
import jax
import jax.numpy as jnp
from jax import lax
from jax.experimental import pallas as pl
from jax.experimental.pallas import tpu as pltpu
from jax.sharding import PartitionSpec as P

C, HID, SIDE, NB = 320, 1280, 16, 8
CP = 384
CELLS = SIDE * SIDE
ROWS = 6656
DOWN, UP, SMALL = 0, 3200, 6400
BF, F32 = jnp.bfloat16, jnp.float32
K0, K1 = 0.7978845608028654, 0.044715
T_LANES = (((1,), (1,)), ((), ()))
T_ROWS = (((0,), (0,)), ((), ()))


def dot(a, b, dims=(((1,), (0,)), ((), ()))):
    return lax.dot_general(a, b, dims, preferred_element_type=F32)


def lane_tile(t):
    return pl.ds(pl.multiple_of(t * 128, 128), 128)


def shift_columns(pad_ref, shift_ref, first, step):
    for dj in range(7):
        at = first + step * dj
        shift_ref[dj] = pad_ref[:, at : at + SIDE, :]


def taps_of(small_ref, b, dj, lanes):
    return [jnp.broadcast_to(small_ref[b, dr * 7 + dj : dr * 7 + dj + 1, lanes], (8, 128)) for dr in range(7)]


def conv_forward(shift_ref, small_ref, b, out_ref):
    def tile(t, _):
        lanes = lane_tile(t)
        for half in range(2):
            cols = pl.ds(8 * half, 8)
            acc = [jnp.broadcast_to(small_ref[b, 49:50, lanes], (8, 128))] * SIDE
            for dj in range(7):
                taps = taps_of(small_ref, b, dj, lanes)
                for r in range(SIDE):
                    x = shift_ref[dj, r, cols, lanes]
                    for dr in range(7):
                        i = r - dr + 3
                        if 0 <= i < SIDE:
                            acc[i] = acc[i] + x * taps[dr]
            for i in range(SIDE):
                out_ref[i, cols, lanes] = acc[i]
        return 0

    lax.fori_loop(0, 3, tile, 0)


def conv_backward(shift_ref, x_ref, small_ref, b, dx_ref, dk_ref):
    def tile(t, _):
        lanes = lane_tile(t)
        for half in range(2):
            cols = pl.ds(8 * half, 8)
            xs = [x_ref[i, cols, lanes] for i in range(SIDE)]
            acc = [None] * SIDE
            for dj in range(7):
                taps = taps_of(small_ref, b, dj, lanes)
                dks = [None] * 7
                for r in range(SIDE):
                    g = shift_ref[dj, r, cols, lanes]
                    for dr in range(7):
                        i = r + dr - 3
                        if 0 <= i < SIDE:
                            p = g * taps[dr]
                            acc[i] = p if acc[i] is None else acc[i] + p
                            p = g * xs[i]
                            dks[dr] = p if dks[dr] is None else dks[dr] + p
                for dr in range(7):
                    if half == 0:
                        dk_ref[dr * 7 + dj, :, lanes] = dks[dr]
                    else:
                        dk_ref[dr * 7 + dj, :, lanes] += dks[dr]
            for i in range(SIDE):
                dx_ref[i, cols, lanes] = acc[i]
        return 0

    lax.fori_loop(0, 3, tile, 0)


def weight_chunk(w_ref, b, base, n):
    at = base + 640 * n
    return jnp.concatenate([w_ref[b, at : at + C, :], w_ref[b, at + C : at + 2 * C, :]], axis=1)


def small_row(small_ref, b, row):
    return small_ref[b, row : row + 1, 0:C]


def up_bias_chunk(small_ref, b, n):
    parts = []
    for t in (2 * n, 2 * n + 1):
        parts.append(small_ref[b, 54 + t // 3 : 55 + t // 3, (t % 3) * 128 : (t % 3 + 1) * 128])
    return jnp.concatenate(parts, axis=1)


def window_of(h):
    cell = lax.broadcasted_iota(jnp.int32, (CELLS, 1), 0)
    return ((cell // SIDE < h) & (cell % SIDE < h)).astype(F32)


def block_forward(b, h, w_ref, small_ref, v_ref, pad_ref, shift_ref, mix_ref, act_ref, slope_ref, xhat_ref, inv_ref, proj_ref):
    v = v_ref[b].astype(F32)
    pad_ref[:, 8:24, 0:C] = v.reshape(SIDE, SIDE, C)
    shift_columns(pad_ref, shift_ref, 5, 1)
    conv_forward(shift_ref, small_ref, b, mix_ref)
    mixed = mix_ref[:, :, 0:C].reshape(CELLS, C)
    center = jnp.sum(mixed, axis=1, keepdims=True) * (1.0 / C)
    mixed = mixed - center
    inv = lax.rsqrt(jnp.sum(mixed * mixed, axis=1, keepdims=True) * (1.0 / C) + 1e-6)
    xhat = mixed * inv
    xhat_ref[b] = xhat
    inv_ref[b] = inv
    normed = (xhat * small_row(small_ref, b, 50) + small_row(small_ref, b, 51)).astype(BF)
    proj = jnp.broadcast_to(small_row(small_ref, b, 52), (CELLS, C))
    for n in range(5):
        cols = slice(256 * n, 256 * n + 256)
        u = dot(normed, weight_chunk(w_ref, b, UP, n)) + up_bias_chunk(small_ref, b, n)
        uu = u * u
        t = jnp.tanh(u * (K0 + (K0 * K1) * uu))
        lift = 0.5 + 0.5 * t
        act = (u * lift).astype(BF)
        slope = lift + (u * (0.5 - 0.5 * t * t)) * (K0 + (3 * K0 * K1) * uu)
        act_ref[b, :, cols] = act
        slope_ref[b, :, cols] = slope.astype(BF)
        proj = proj + dot(act, weight_chunk(w_ref, b, DOWN, n), T_LANES)
    proj_ref[b] = proj.astype(BF)
    out = (v + small_row(small_ref, b, 53) * proj) * window_of(h)
    return out.astype(BF)


def products_backward(b, h, g_ref, w_ref, small_ref, pad_ref, act_ref, slope_ref, xhat_ref, inv_ref, proj_ref, sg_ref):
    g = g_ref[...] * window_of(h)
    g_ref[...] = g
    sg_ref[53:54, 0:C] = jnp.sum(g * proj_ref[b].astype(F32), axis=0, keepdims=True)
    dproj = g * small_row(small_ref, b, 53)
    sg_ref[52:53, 0:C] = jnp.sum(dproj, axis=0, keepdims=True)
    dproj = dproj.astype(BF)
    xhat = xhat_ref[b]
    gain = small_row(small_ref, b, 50)
    normed = (xhat * gain + small_row(small_ref, b, 51)).astype(BF)
    dnormed = None
    for n in range(5):
        cols = slice(256 * n, 256 * n + 256)
        dact = dot(dproj, weight_chunk(w_ref, b, DOWN, n))
        dhid = dact * slope_ref[b, :, cols].astype(F32)
        bias = jnp.sum(dhid, axis=0, keepdims=True)
        dhid = dhid.astype(BF)
        part = dot(dhid, weight_chunk(w_ref, b, UP, n), T_LANES)
        dnormed = part if dnormed is None else dnormed + part
        dup = dot(normed, dhid, T_ROWS).astype(BF)
        ddown = dot(dproj, act_ref[b, :, cols], T_ROWS).astype(BF)
        for k in range(2):
            t = 2 * n + k
            lanes = slice(128 * k, 128 * k + 128)
            w_ref[b, UP + C * t : UP + C * t + C, :] = dup[:, lanes]
            w_ref[b, DOWN + C * t : DOWN + C * t + C, :] = ddown[:, lanes]
            sg_ref[54 + t // 3 : 55 + t // 3, (t % 3) * 128 : (t % 3 + 1) * 128] = bias[:, lanes]
    sg_ref[50:51, 0:C] = jnp.sum(dnormed * xhat, axis=0, keepdims=True)
    sg_ref[51:52, 0:C] = jnp.sum(dnormed, axis=0, keepdims=True)
    dxhat = dnormed * gain
    m0 = jnp.sum(dxhat, axis=1, keepdims=True) * (1.0 / C)
    m1 = jnp.sum(dxhat * xhat, axis=1, keepdims=True) * (1.0 / C)
    dmixed = inv_ref[b] * (dxhat - m0 - xhat * m1)
    sg_ref[49:50, 0:C] = jnp.sum(dmixed, axis=0, keepdims=True)
    pad_ref[:, 8:24, 0:C] = dmixed.reshape(SIDE, SIDE, C)


def spatial_backward(b, g_ref, w_ref, small_ref, v_ref, pad_ref, shift_ref, mix_ref, x_ref, dk_ref, sg_ref):
    x_ref[:, :, 0:C] = v_ref[b].astype(F32).reshape(SIDE, SIDE, C)
    shift_columns(pad_ref, shift_ref, 11, -1)
    conv_backward(shift_ref, x_ref, small_ref, b, mix_ref, dk_ref)
    sg_ref[0:49, :] = jnp.sum(dk_ref[...], axis=1)
    for j in range(3):
        w_ref[b, SMALL + 64 * j : SMALL + 64 * j + 64, :] = sg_ref[:, 128 * j : 128 * j + 128].astype(BF)
    g_ref[...] = (g_ref[...] + mix_ref[:, :, 0:C].reshape(CELLS, C)).astype(BF).astype(F32)


def pack_small(dw_kernel, dw_bias, gain, nbias, up_bias, down_bias, scale):
    n = dw_kernel.shape[0]
    rows = jnp.concatenate([dw_kernel.reshape(n, 49, C), dw_bias[:, None], gain[:, None], nbias[:, None], down_bias[:, None], scale[:, None]], axis=1)
    rows = jnp.pad(rows, ((0, 0), (0, 0), (0, CP - C)))
    up = jnp.pad(up_bias, ((0, 0), (0, 4 * CP - HID))).reshape(n, 4, CP)
    return jnp.concatenate([rows, up, jnp.zeros((n, 6, CP), F32)], axis=1)


MESH = pl.DeviceIdType.MESH


class Place:
    def __init__(self):
        s, d = lax.axis_index("section"), lax.axis_index("dp")
        self.s, self.d = s, d
        self.core = d % 2
        self.z = (d // 32) * 4 + s
        self.step1 = 2 + 6 * self.core
        self.step2 = 10 - self.step1
        self.f1 = (d // self.step1) % 4
        self.f2 = (d // self.step2) % 4
        self.x, self.y = (d // 2) % 4, (d // 8) % 4
        self.color = (self.x + self.y) % 2

    def sibling(self):
        return (self.s, self.d + 1 - 2 * self.core)

    def first(self, k):
        q = (self.f1 + k) % 4
        return q, (self.s, self.d + (q - self.f1) * self.step1)

    def second(self, k):
        q = (self.f2 + k) % 4
        return q, (self.s, self.d + (q - self.f2) * self.step2)

    def beside(self, side):
        step, at = (2, self.x) if side < 2 else (8, self.y)
        k = 1 if side % 2 == 0 else 3
        return (self.s, self.d + ((at + k) % 4 - at) * step)

    def up_z(self, k):
        z = (self.z + k) % 8
        return (z % 4, (z // 4) * 32 + self.d % 32)


def greet(devices):
    barrier = pltpu.get_barrier_semaphore()
    for device in devices:
        pl.semaphore_signal(barrier, inc=1, device_id=device, device_id_type=MESH)
    pl.semaphore_wait(barrier, len(devices))


def remote(src, dst, send, recv, device):
    return pltpu.make_async_remote_copy(src_ref=src, dst_ref=dst, send_sem=send, recv_sem=recv, device_id=device, device_id_type=MESH)


def add_rows(dst_ref, b, base, count, src_refs):
    step = next(n for n in (256, 224, 208, 192, 112, 96) if count % n == 0)

    def add(i, _):
        rows = pl.ds(pl.multiple_of(base + i * step, 16), step)
        own = pl.ds(pl.multiple_of(i * step, 16), step)
        total = dst_ref[b, rows, :].astype(F32)
        for src in src_refs:
            total = total + src[own, :].astype(F32)
        dst_ref[b, rows, :] = total.astype(BF)
        return 0

    lax.fori_loop(0, count // step, add, 0)


class Reduce:
    def __init__(self, at, part, g_ref, outs, fin_ref, cr, xr, yr, zr, sems):
        self.at, self.part, self.g, self.fin = at, part, g_ref, fin_ref
        self.up, self.down, self.small = outs
        self.cr, self.xr, self.yr, self.zr = cr, xr, yr, zr
        self.sems = sems
        self.start = 3072 * part
        self.half = 1536 + 256 * part
        self.quarter, self.piece_rows = self.half // 4, self.half // 16
        self.side = self.quarter // 2
        self.mine = self.start + at.core * self.half

    def rows(self, at, count):
        return pl.ds(pl.multiple_of(at, 16), count)

    def core_copy(self, b):
        at, (s, r) = self.at, self.sems[0]
        other = self.start + (1 - at.core) * self.half
        return remote(self.g.at[b, self.rows(other, self.half)], self.cr.at[b, pl.ds(self.start // 2, self.half)], s.at[self.part, b], r.at[self.part, b], at.sibling())

    def first_copy(self, b, n):
        at, (s, r) = self.at, self.sems[1]
        quarter, high, k = ((2, 0, 1), (2, 1, 3), (1, 1, 1), (3, 0, 3), (1, 0, 1), (3, 1, 3))[n]
        rows = self.rows(self.mine + ((at.f1 + quarter) % 4) * self.quarter + high * self.side, self.side)
        return remote(self.g.at[b, rows], self.xr.at[b, n, pl.ds(192 * self.part, self.side)], s.at[self.part, b, n], r.at[self.part, b, n], at.first(k)[1])

    def second_copy(self, b, k):
        at, (s, r) = self.at, self.sems[2]
        q, device = at.second(k)
        rows = self.rows(self.mine + at.f1 * self.quarter + q * self.piece_rows, self.piece_rows)
        return remote(self.g.at[b, rows], self.yr.at[b, k - 1, pl.ds(96 * self.part, self.piece_rows)], s.at[self.part, b, k - 1], r.at[self.part, b, k - 1], device)

    def piece(self):
        at = self.at
        return self.rows(self.mine + at.f1 * self.quarter + at.f2 * self.piece_rows, self.piece_rows)

    def z_copy(self, b, hi, source):
        at, (s, r) = self.at, self.sems[3]
        device = (b % 4, hi * 32 + at.d % 32)
        return remote(self.g.at[b, self.piece()], self.zr.at[b // 4, source, pl.ds(96 * self.part, self.piece_rows)], s.at[self.part, b, hi], r.at[self.part, b // 4, source], device)

    def back_second(self, l, k, arriving):
        at, (s, r) = self.at, self.sems[4]
        device = at.second(k)[1]
        q = at.second(4 - k)[0] if arriving else at.f2
        rows = self.fin.at[l, self.rows(self.mine + at.f1 * self.quarter + q * self.piece_rows, self.piece_rows)]
        return remote(rows, rows, s.at[self.part, l, k - 1], r.at[self.part, l, k - 1], device)

    def back_first(self, l, k, arriving):
        at, (s, r) = self.at, self.sems[5]
        device = at.first(k)[1]
        q = at.first(4 - k)[0] if arriving else at.f1
        rows = self.fin.at[l, self.rows(self.mine + q * self.quarter, self.quarter)]
        return remote(rows, rows, s.at[self.part, l, k - 1], r.at[self.part, l, k - 1], device)

    def back_core(self, l, core):
        at, (s, r) = self.at, self.sems[6]
        rows = self.fin.at[l, self.rows(self.start + core * self.half, self.half)]
        return remote(rows, rows, s.at[self.part, l], r.at[self.part, l], at.sibling())

    def stage0(self, b):
        self.core_copy(b).start()

    def stage1(self, b):
        self.core_copy(b).wait()
        add_rows(self.g, b, self.mine, self.half, [self.cr.at[b, pl.ds(self.start // 2, self.half)]])
        for n in range(4):
            self.first_copy(b, n).start()

    def stage2(self, b):
        at = self.at
        for n in range(2):
            self.first_copy(b, n).wait_recv()
            quarter, high = ((1, 0), (3, 1))[n]
            base = self.mine + ((at.f1 + quarter) % 4) * self.quarter + high * self.side
            add_rows(self.g, b, base, self.side, [self.xr.at[b, n, pl.ds(192 * self.part, self.side)]])
            self.first_copy(b, 4 + n).start()

    def stage3(self, b):
        at = self.at
        for n in range(6):
            self.first_copy(b, n).wait_send()
        for n in range(2, 6):
            self.first_copy(b, n).wait_recv()
        base = self.mine + at.f1 * self.quarter
        for high, (one, two) in enumerate(((3, 4), (2, 5))):
            add_rows(self.g, b, base + high * self.side, self.side, [self.xr.at[b, n, pl.ds(192 * self.part, self.side)] for n in (one, two)])
        for k in (2, 1, 3):
            self.second_copy(b, k).start()

    def stage4(self, b):
        at = self.at
        for k in (1, 2, 3):
            self.second_copy(b, k).wait()
        base = self.mine + at.f1 * self.quarter + at.f2 * self.piece_rows
        add_rows(self.g, b, base, self.piece_rows, [self.yr.at[b, k, pl.ds(96 * self.part, self.piece_rows)] for k in range(3)])
        for hi in range(2):
            @pl.when(at.z != hi * 4 + b % 4)
            def _():
                self.z_copy(b, hi, at.z).start()

    def stage5(self, b):
        at = self.at
        for hi in range(2):
            @pl.when(at.z != hi * 4 + b % 4)
            def _():
                self.z_copy(b, hi, at.z).wait_send()

        @pl.when(at.s == b % 4)
        def _():
            l = b // 4
            for k in range(1, 8):
                self.z_copy(b, 0, (at.z + k) % 8).wait_recv()
            rows = pl.ds(96 * self.part, self.piece_rows)
            self.zr[l, at.z, rows, :] = self.g[b, self.piece(), :]
            total = self.zr[l, 0, rows, :].astype(F32)
            for z in range(1, 8):
                total = total + self.zr[l, z, rows, :].astype(F32)
            self.fin[l, self.piece(), :] = total.astype(BF)
            for k in (2, 1, 3):
                self.back_second(l, k, False).start()

    def stage6(self, b):
        @pl.when(self.at.s == b % 4)
        def _():
            l = b // 4
            for k in (1, 2, 3):
                self.back_second(l, k, False).wait_send()
                self.back_second(l, k, True).wait_recv()
            for k in (2, 1, 3):
                self.back_first(l, k, False).start()

    def stage7(self, b):
        at = self.at

        @pl.when(at.s == b % 4)
        def _():
            l = b // 4
            for k in (1, 2, 3):
                self.back_first(l, k, False).wait_send()
                self.back_first(l, k, True).wait_recv()
            self.back_core(l, at.core).start()

    def stage8(self, b):
        at = self.at

        @pl.when(at.s == b % 4)
        def _():
            l = b // 4
            self.back_core(l, at.core).wait_send()
            self.back_core(l, 1 - at.core).wait_recv()
            if self.part == 0:
                return
            for t in range(10):
                lanes = slice(128 * t, 128 * t + 128)
                self.up[l, :, lanes] = self.fin[l, UP + C * t : UP + C * t + C, :]
                self.down[l, :, lanes] = self.fin[l, DOWN + C * t : DOWN + C * t + C, :]
            for t in range(3):
                self.small[l, :, 128 * t : 128 * t + 128] = self.fin[l, SMALL + 64 * t : SMALL + 64 * t + 64, :].astype(F32)

    def stages(self):
        return [self.stage0, self.stage1, self.stage2, self.stage3, self.stage4, self.stage5, self.stage6, self.stage7, self.stage8]


def pair(*shape):
    return [pltpu.SemaphoreType.DMA(shape), pltpu.SemaphoreType.DMA(shape)]


def reduce_scratch():
    buffers = [
        pltpu.VMEM((2, ROWS, 128), BF),
        pltpu.VMEM((NB, ROWS // 2, 128), BF),
        pltpu.VMEM((NB, 6, ROWS // 16, 128), BF),
        pltpu.VMEM((NB, 3, ROWS // 32, 128), BF),
        pltpu.VMEM((2, 8, ROWS // 32, 128), BF),
    ]
    sems = pair(2, NB) + pair(2, NB, 6) + pair(2, NB, 3)
    sems += [pltpu.SemaphoreType.DMA((2, NB, 2)), pltpu.SemaphoreType.DMA((2, 2, 8))]
    sems += pair(2, 2, 3) + pair(2, 2, 3) + pair(2, 2)
    return buffers + sems


def make_reduce(at, part, g_ref, outs, refs):
    sems = [tuple(refs[5 + 2 * i : 7 + 2 * i]) for i in range(7)]
    return Reduce(at, part, g_ref, outs, *refs[:5], sems)


WHALF, SHARE, PART = 3200, 1600, 400


class Gather:
    def __init__(self, at, w_ref, small_ref, sems):
        self.at, self.w, self.small_ref = at, w_ref, small_ref
        self.zs, self.ps, self.cs, self.small_zs, self.small_cs = sems

    def block(self, l, kind):
        return l * 4 + (self.at.s + (3, 1, 2)[kind]) % 4

    def share(self, core, color):
        return pl.multiple_of(core * WHALF + color * SHARE, 16)

    def along_z(self, l, b, kind, device):
        at = self.at
        w = self.w.at[b, pl.ds(self.share(at.core, at.color), SHARE)]
        small = self.small_ref.at[b, pl.ds(pl.multiple_of(at.core * 32, 32), 32)]
        return [
            remote(w, w, self.zs[0].at[l, kind], self.zs[1].at[l, kind], device),
            remote(small, small, self.small_zs[0].at[l, kind], self.small_zs[1].at[l, kind], device),
        ]

    def in_plane(self, l, kind, side, color):
        at = self.at
        w = self.w.at[self.block(l, kind), pl.ds(pl.multiple_of(self.share(at.core, color) + side * PART, 16), PART)]
        return remote(w, w, self.ps[0].at[l, kind, side], self.ps[1].at[l, kind, side], at.beside(side))

    def to_sibling(self, l, kind, core, color, which):
        w = self.w.at[self.block(l, kind), pl.ds(self.share(core, color), SHARE)]
        return remote(w, w, self.cs[0].at[l, kind, which], self.cs[1].at[l, kind, which], self.at.sibling())

    def small_to_sibling(self, l, kind, core):
        small = self.small_ref.at[self.block(l, kind), pl.ds(pl.multiple_of(core * 32, 32), 32)]
        return remote(small, small, self.small_cs[0].at[l, kind], self.small_cs[1].at[l, kind], self.at.sibling())

    def begin(self, l):
        at = self.at
        for kind, k in ((0, 1), (1, -1)):
            for c in self.along_z(l, l * 4 + at.s, kind, at.up_z(k)):
                c.start()

    def spread(self, l, kind):
        at = self.at
        for side in range(4):
            self.in_plane(l, kind, side, at.color).start()
        self.to_sibling(l, kind, at.core, at.color, 0).start()
        self.small_to_sibling(l, kind, at.core).start()

    def near(self, l):
        at = self.at
        for kind, k in ((0, -1), (1, 1)):
            b = self.block(l, kind)
            for c in self.along_z(l, b, kind, at.up_z(k)):
                c.wait_recv()

            @pl.when(at.core == 1 - kind)
            def _():
                for c in self.along_z(l, b, 2, at.up_z(-k)):
                    c.start()
        for kind in range(2):
            self.spread(l, kind)

    def close_plane(self, l, kind):
        at = self.at
        for side in range(4):
            self.in_plane(l, kind, side, 1 - at.color).wait_recv()
        self.to_sibling(l, kind, at.core, 1 - at.color, 1).start()

    def far(self, l):
        at = self.at
        for c in self.along_z(l, self.block(l, 2), 2, at.up_z(1)):
            c.wait_recv()
        self.spread(l, 2)
        for kind in range(2):
            self.close_plane(l, kind)

    def last(self, l):
        at = self.at
        self.close_plane(l, 2)
        for kind in range(3):
            self.to_sibling(l, kind, 1 - at.core, at.color, 0).wait_recv()
            self.to_sibling(l, kind, 1 - at.core, 1 - at.color, 1).wait_recv()
            self.small_to_sibling(l, kind, 1 - at.core).wait_recv()

    def drain(self, l):
        at = self.at
        for kind in range(3):
            for c in self.along_z(l, self.block(l, kind), kind, at.up_z(1)):
                c.wait_send()
            for side in range(4):
                self.in_plane(l, kind, side, at.color).wait_send()
            self.to_sibling(l, kind, at.core, at.color, 0).wait_send()
            self.to_sibling(l, kind, at.core, 1 - at.color, 1).wait_send()
            self.small_to_sibling(l, kind, at.core).wait_send()


def gather_scratch():
    return pair(2, 3) + pair(2, 3, 4) + pair(2, 3, 2) + pair(2, 3) + pair(2, 3)


def make_gather(at, w_ref, small_ref, sems):
    return Gather(at, w_ref, small_ref, [tuple(sems[2 * i : 2 * i + 2]) for i in range(5)])


def clear(ref):
    ref[...] = jnp.zeros(ref.shape, ref.dtype)


def step_kernel(heights_ref, images_ref, cot_ref, up_in, down_in, small_in, up_out, down_out, small_out, w_ref, small_ref, image_ref, v_ref, pad_ref, shift_ref, mix_ref, x_ref, act_ref, slope_ref, xhat_ref, inv_ref, proj_ref, dk_ref, sg_ref, g_ref, load_sem, own_sem, *refs):
    at = Place()
    gather = make_gather(at, w_ref, small_ref, refs[:10])
    units = [make_reduce(at, part, w_ref, (up_out, down_out, small_out), refs[10:]) for part in range(2)]
    own = [[], []]
    for l in range(2):
        b = l * 4 + at.s
        for t in range(10):
            lanes = pl.ds(128 * t, 128)
            own[l].append(pltpu.make_async_copy(up_in.at[l, :, lanes], w_ref.at[b, pl.ds(UP + C * t, C)], own_sem.at[l, t]))
            own[l].append(pltpu.make_async_copy(down_in.at[l, :, lanes], w_ref.at[b, pl.ds(DOWN + C * t, C)], own_sem.at[l, 10 + t]))
        own[l].append(pltpu.make_async_copy(small_in.at[l], small_ref.at[b], own_sem.at[l, 20]))
    load = [pltpu.make_async_copy(images_ref.at[at.s, 0], image_ref.at[0], load_sem.at[0]), pltpu.make_async_copy(cot_ref.at[at.s, 0], image_ref.at[1], load_sem.at[1])]
    for c in own[0] + own[1] + load:
        c.start()
    greet([at.sibling()] + [at.first(k)[1] for k in (1, 2, 3)] + [at.second(k)[1] for k in (1, 2, 3)] + [at.up_z(k) for k in range(1, 8)])
    for c in own[0]:
        c.wait()
    gather.begin(0)
    clear(pad_ref)
    clear(x_ref)
    clear(sg_ref)
    h = heights_ref[at.s]
    for c in load + own[1]:
        c.wait()
    v_ref[0] = (image_ref[0].astype(F32).reshape(CELLS, C) * window_of(h)).astype(BF)
    gather.near(0)
    gather.begin(1)
    gather.far(0)
    gather.last(0)

    def forward(b, _):
        v_ref[b + 1] = block_forward(b, h, w_ref, small_ref, v_ref, pad_ref, shift_ref, mix_ref, act_ref, slope_ref, xhat_ref, inv_ref, proj_ref)
        for n, part in ((1, gather.near), (2, gather.far), (3, gather.last)):
            @pl.when(b == n)
            def _():
                part(1)
        return 0

    lax.fori_loop(0, NB, forward, 0)
    gather.drain(0)
    gather.drain(1)
    g_ref[...] = image_ref[1].astype(F32).reshape(CELLS, C)
    stages = [unit.stages() for unit in units]
    depth = len(stages[0])

    def run_stages(t, first):
        for n in range(depth):
            ago = n - first
            b = NB - 1 - t + (ago + 1) // 2

            @pl.when((b >= 0) & (b < NB))
            def _():
                stages[ago % 2][n](b)

    def tick(t, _):
        b = NB - 1 - t

        @pl.when(b >= 0)
        def _():
            w_ref[b, ROWS - 64 : ROWS, :] = jnp.zeros((64, 128), BF)
            products_backward(b, h, g_ref, w_ref, small_ref, pad_ref, act_ref, slope_ref, xhat_ref, inv_ref, proj_ref, sg_ref)
        run_stages(t, 0)

        @pl.when(b >= 0)
        def _():
            spatial_backward(b, g_ref, w_ref, small_ref, v_ref, pad_ref, shift_ref, mix_ref, x_ref, dk_ref, sg_ref)
        run_stages(t, 1)
        return 0

    lax.fori_loop(0, NB + depth // 2, tick, 0)


def step(heights, images, cotangent, up, down, small):
    hbm = pl.BlockSpec(memory_space=pl.ANY)
    vm = pl.BlockSpec(memory_space=pltpu.VMEM)
    scratch = [
        pltpu.VMEM((NB, ROWS, 128), BF),
        pltpu.VMEM((NB, 64, CP), F32),
        pltpu.VMEM((2, SIDE, SIDE, C), BF),
        pltpu.VMEM((NB + 1, CELLS, C), BF),
        pltpu.VMEM((SIDE, 32, CP), F32),
        pltpu.VMEM((7, SIDE, SIDE, CP), F32),
        pltpu.VMEM((SIDE, SIDE, CP), F32),
        pltpu.VMEM((SIDE, SIDE, CP), F32),
        pltpu.VMEM((NB, CELLS, HID), BF),
        pltpu.VMEM((NB, CELLS, HID), BF),
        pltpu.VMEM((NB, CELLS, C), F32),
        pltpu.VMEM((NB, CELLS, 1), F32),
        pltpu.VMEM((NB, CELLS, C), BF),
        pltpu.VMEM((49, 8, CP), F32),
        pltpu.VMEM((64, CP), F32),
        pltpu.VMEM((CELLS, C), F32),
        pltpu.SemaphoreType.DMA((2,)),
        pltpu.SemaphoreType.DMA((2, 21)),
    ]
    return pl.pallas_call(
        step_kernel,
        out_shape=(jax.ShapeDtypeStruct((2, C, HID), BF), jax.ShapeDtypeStruct((2, C, HID), BF), jax.ShapeDtypeStruct((2, 64, CP), F32)),
        in_specs=[pl.BlockSpec(memory_space=pltpu.SMEM)] + [hbm] * 5,
        out_specs=(vm, vm, vm),
        scratch_shapes=scratch + gather_scratch() + reduce_scratch(),
        compiler_params=pltpu.CompilerParams(collective_id=0, has_side_effects=True, vmem_limit_bytes=62 * 2**20),
        cost_estimate=pl.CostEstimate(flops=12 * 10**9, bytes_accessed=30 * 10**6, transcendentals=3 * 10**6),
    )(heights, images, cotangent, up, down, small)


def body(images, cotangent, heights, dw_kernel, dw_bias, norm_gain, norm_bias, up_weight, up_bias, down_weight, down_bias, layer_scale):
    small = pack_small(*(a[:, 0] for a in (dw_kernel, dw_bias, norm_gain, norm_bias, up_bias, down_bias, layer_scale)))
    up, down, small = step(heights, images, cotangent, up_weight[:, 0], down_weight[:, 0].swapaxes(1, 2), small)
    row = lambda i: small[:, i, :C]
    up_bias_grad = small[:, 54:58].reshape(2, 4 * CP)[:, :HID]
    parts = (small[:, :49, :C].reshape(2, 7, 7, C), row(49), row(50), row(51), up, up_bias_grad, down.swapaxes(1, 2), row(52), row(53))
    return tuple(p[:, None] for p in parts)


def solution(mesh):
    three, two = P(None, "section", None, None), P(None, "section", None)
    five = P(None, "section", None, None, None)
    image = P(None, "dp", None, None, None)
    weights = (five, two, two, two, three, two, three, two, two)
    return jax.shard_map(body, mesh=mesh, in_specs=(image, image, P()) + weights, out_specs=weights, check_vma=False)
```

```python
import jax
import jax.numpy as jnp
from jax import lax
from jax.experimental import pallas as pl
from jax.experimental.pallas import tpu as pltpu
from jax.sharding import PartitionSpec as P

C, HID, SIDE, NB = 320, 1280, 16, 8
CP = 384
CELLS = SIDE * SIDE
ROWS = 6656
DOWN, UP, SMALL = 0, 3200, 6400
BF, F32 = jnp.bfloat16, jnp.float32
K0, K1 = 0.7978845608028654, 0.044715
T_LANES = (((1,), (1,)), ((), ()))
T_ROWS = (((0,), (0,)), ((), ()))


def dot(a, b, dims=(((1,), (0,)), ((), ()))):
    return lax.dot_general(a, b, dims, preferred_element_type=F32)


def lane_tile(t):
    return pl.ds(pl.multiple_of(t * 128, 128), 128)


def shift_columns(pad_ref, shift_ref, first, step):
    for dj in range(7):
        at = first + step * dj
        shift_ref[dj] = pad_ref[:, at : at + SIDE, :]


def taps_of(small_ref, b, dj, lanes):
    return [jnp.broadcast_to(small_ref[b, dr * 7 + dj : dr * 7 + dj + 1, lanes], (8, 128)) for dr in range(7)]


def conv_forward(shift_ref, small_ref, b, out_ref):
    def tile(t, _):
        lanes = lane_tile(t)
        for half in range(2):
            cols = pl.ds(8 * half, 8)
            acc = [jnp.broadcast_to(small_ref[b, 49:50, lanes], (8, 128))] * SIDE
            for dj in range(7):
                taps = taps_of(small_ref, b, dj, lanes)
                for r in range(SIDE):
                    x = shift_ref[dj, r, cols, lanes]
                    for dr in range(7):
                        i = r - dr + 3
                        if 0 <= i < SIDE:
                            acc[i] = acc[i] + x * taps[dr]
            for i in range(SIDE):
                out_ref[i, cols, lanes] = acc[i]
        return 0

    lax.fori_loop(0, 3, tile, 0)


def conv_backward(shift_ref, x_ref, small_ref, b, dx_ref, dk_ref):
    def tile(t, _):
        lanes = lane_tile(t)
        for half in range(2):
            cols = pl.ds(8 * half, 8)
            xs = [x_ref[i, cols, lanes] for i in range(SIDE)]
            acc = [None] * SIDE
            for dj in range(7):
                taps = taps_of(small_ref, b, dj, lanes)
                dks = [None] * 7
                for r in range(SIDE):
                    g = shift_ref[dj, r, cols, lanes]
                    for dr in range(7):
                        i = r + dr - 3
                        if 0 <= i < SIDE:
                            p = g * taps[dr]
                            acc[i] = p if acc[i] is None else acc[i] + p
                            p = g * xs[i]
                            dks[dr] = p if dks[dr] is None else dks[dr] + p
                for dr in range(7):
                    if half == 0:
                        dk_ref[dr * 7 + dj, :, lanes] = dks[dr]
                    else:
                        dk_ref[dr * 7 + dj, :, lanes] += dks[dr]
            for i in range(SIDE):
                dx_ref[i, cols, lanes] = acc[i]
        return 0

    lax.fori_loop(0, 3, tile, 0)


def weight_chunk(w_ref, b, base, n):
    at = base + 640 * n
    return jnp.concatenate([w_ref[b, at : at + C, :], w_ref[b, at + C : at + 2 * C, :]], axis=1)


def small_row(small_ref, b, row):
    return small_ref[b, row : row + 1, 0:C]


def up_bias_chunk(small_ref, b, n):
    parts = []
    for t in (2 * n, 2 * n + 1):
        parts.append(small_ref[b, 54 + t // 3 : 55 + t // 3, (t % 3) * 128 : (t % 3 + 1) * 128])
    return jnp.concatenate(parts, axis=1)


def window_of(h):
    cell = lax.broadcasted_iota(jnp.int32, (CELLS, 1), 0)
    return ((cell // SIDE < h) & (cell % SIDE < h)).astype(F32)


def spatial_forward(b, small_ref, v_ref, pad_ref, shift_ref, mix_ref, xhat_ref, inv_ref):
    pad_ref[:, 8:24, 0:C] = v_ref[b].astype(F32).reshape(SIDE, SIDE, C)
    shift_columns(pad_ref, shift_ref, 5, 1)
    conv_forward(shift_ref, small_ref, b, mix_ref)
    mixed = mix_ref[:, :, 0:C].reshape(CELLS, C)
    center = jnp.sum(mixed, axis=1, keepdims=True) * (1.0 / C)
    mixed = mixed - center
    inv = lax.rsqrt(jnp.sum(mixed * mixed, axis=1, keepdims=True) * (1.0 / C) + 1e-6)
    xhat_ref[b] = mixed * inv
    inv_ref[b] = inv


def products_forward(b, h, w_ref, small_ref, v_ref, act_ref, slope_ref, xhat_ref, proj_ref):
    xhat = xhat_ref[b]
    normed = (xhat * small_row(small_ref, b, 50) + small_row(small_ref, b, 51)).astype(BF)
    proj = jnp.broadcast_to(small_row(small_ref, b, 52), (CELLS, C))
    for n in range(5):
        cols = slice(256 * n, 256 * n + 256)
        u = dot(normed, weight_chunk(w_ref, b, UP, n)) + up_bias_chunk(small_ref, b, n)
        uu = u * u
        t = jnp.tanh(u * (K0 + (K0 * K1) * uu))
        lift = 0.5 + 0.5 * t
        act = (u * lift).astype(BF)
        slope = lift + (u * (0.5 - 0.5 * t * t)) * (K0 + (3 * K0 * K1) * uu)
        act_ref[b, :, cols] = act
        slope_ref[b, :, cols] = slope.astype(BF)
        proj = proj + dot(act, weight_chunk(w_ref, b, DOWN, n), T_LANES)
    proj_ref[b] = proj.astype(BF)
    out = (v_ref[b].astype(F32) + small_row(small_ref, b, 53) * proj) * window_of(h)
    v_ref[b + 1] = out.astype(BF)


def products_backward(b, h, g_ref, w_ref, small_ref, pad_ref, act_ref, slope_ref, xhat_ref, inv_ref, proj_ref, sg_ref):
    g = g_ref[...] * window_of(h)
    g_ref[...] = g
    sg_ref[53:54, 0:C] = jnp.sum(g * proj_ref[b].astype(F32), axis=0, keepdims=True)
    dproj = g * small_row(small_ref, b, 53)
    sg_ref[52:53, 0:C] = jnp.sum(dproj, axis=0, keepdims=True)
    dproj = dproj.astype(BF)
    xhat = xhat_ref[b]
    gain = small_row(small_ref, b, 50)
    normed = (xhat * gain + small_row(small_ref, b, 51)).astype(BF)
    dnormed = None
    for n in range(5):
        cols = slice(256 * n, 256 * n + 256)
        dact = dot(dproj, weight_chunk(w_ref, b, DOWN, n))
        dhid = dact * slope_ref[b, :, cols].astype(F32)
        bias = jnp.sum(dhid, axis=0, keepdims=True)
        dhid = dhid.astype(BF)
        part = dot(dhid, weight_chunk(w_ref, b, UP, n), T_LANES)
        dnormed = part if dnormed is None else dnormed + part
        dup = dot(normed, dhid, T_ROWS).astype(BF)
        ddown = dot(dproj, act_ref[b, :, cols], T_ROWS).astype(BF)
        for k in range(2):
            t = 2 * n + k
            lanes = slice(128 * k, 128 * k + 128)
            w_ref[b, UP + C * t : UP + C * t + C, :] = dup[:, lanes]
            w_ref[b, DOWN + C * t : DOWN + C * t + C, :] = ddown[:, lanes]
            sg_ref[54 + t // 3 : 55 + t // 3, (t % 3) * 128 : (t % 3 + 1) * 128] = bias[:, lanes]
    sg_ref[50:51, 0:C] = jnp.sum(dnormed * xhat, axis=0, keepdims=True)
    sg_ref[51:52, 0:C] = jnp.sum(dnormed, axis=0, keepdims=True)
    dxhat = dnormed * gain
    m0 = jnp.sum(dxhat, axis=1, keepdims=True) * (1.0 / C)
    m1 = jnp.sum(dxhat * xhat, axis=1, keepdims=True) * (1.0 / C)
    dmixed = inv_ref[b] * (dxhat - m0 - xhat * m1)
    sg_ref[49:50, 0:C] = jnp.sum(dmixed, axis=0, keepdims=True)
    pad_ref[:, 8:24, 0:C] = dmixed.reshape(SIDE, SIDE, C)


def spatial_backward(b, g_ref, w_ref, small_ref, v_ref, pad_ref, shift_ref, mix_ref, x_ref, dk_ref, sg_ref):
    x_ref[:, :, 0:C] = v_ref[b].astype(F32).reshape(SIDE, SIDE, C)
    shift_columns(pad_ref, shift_ref, 11, -1)
    conv_backward(shift_ref, x_ref, small_ref, b, mix_ref, dk_ref)
    sg_ref[0:49, :] = jnp.sum(dk_ref[...], axis=1)
    for j in range(3):
        w_ref[b, SMALL + 64 * j : SMALL + 64 * j + 64, :] = sg_ref[:, 128 * j : 128 * j + 128].astype(BF)
    g_ref[...] = (g_ref[...] + mix_ref[:, :, 0:C].reshape(CELLS, C)).astype(BF).astype(F32)


def pack_small(dw_kernel, dw_bias, gain, nbias, up_bias, down_bias, scale):
    n = dw_kernel.shape[0]
    rows = jnp.concatenate([dw_kernel.reshape(n, 49, C), dw_bias[:, None], gain[:, None], nbias[:, None], down_bias[:, None], scale[:, None]], axis=1)
    rows = jnp.pad(rows, ((0, 0), (0, 0), (0, CP - C)))
    up = jnp.pad(up_bias, ((0, 0), (0, 4 * CP - HID))).reshape(n, 4, CP)
    return jnp.concatenate([rows, up, jnp.zeros((n, 6, CP), F32)], axis=1)


MESH = pl.DeviceIdType.MESH


class Place:
    def __init__(self):
        s, d = lax.axis_index("section"), lax.axis_index("dp")
        self.s, self.d = s, d
        self.core = d % 2
        self.z = (d // 32) * 4 + s
        self.step1 = 2 + 6 * self.core
        self.step2 = 10 - self.step1
        self.f1 = (d // self.step1) % 4
        self.f2 = (d // self.step2) % 4
        self.x, self.y = (d // 2) % 4, (d // 8) % 4
        self.color = (self.x + self.y) % 2

    def sibling(self):
        return (self.s, self.d + 1 - 2 * self.core)

    def first(self, k):
        q = (self.f1 + k) % 4
        return q, (self.s, self.d + (q - self.f1) * self.step1)

    def second(self, k):
        q = (self.f2 + k) % 4
        return q, (self.s, self.d + (q - self.f2) * self.step2)

    def beside(self, side):
        step, at = (2, self.x) if side < 2 else (8, self.y)
        k = 1 if side % 2 == 0 else 3
        return (self.s, self.d + ((at + k) % 4 - at) * step)

    def up_z(self, k):
        z = (self.z + k) % 8
        return (z % 4, (z // 4) * 32 + self.d % 32)


def greet(devices):
    barrier = pltpu.get_barrier_semaphore()
    for device in devices:
        pl.semaphore_signal(barrier, inc=1, device_id=device, device_id_type=MESH)
    pl.semaphore_wait(barrier, len(devices))


def remote(src, dst, send, recv, device):
    return pltpu.make_async_remote_copy(src_ref=src, dst_ref=dst, send_sem=send, recv_sem=recv, device_id=device, device_id_type=MESH)


def add_rows(dst_ref, b, base, count, src_refs):
    step = next(n for n in (256, 224, 208, 192, 112, 96) if count % n == 0)

    def add(i, _):
        rows = pl.ds(pl.multiple_of(base + i * step, 16), step)
        own = pl.ds(pl.multiple_of(i * step, 16), step)
        total = dst_ref[b, rows, :].astype(F32)
        for src in src_refs:
            total = total + src[own, :].astype(F32)
        dst_ref[b, rows, :] = total.astype(BF)
        return 0

    lax.fori_loop(0, count // step, add, 0)


PACE_LATE = (0, 1, 3, 5, 7, 9, 10, 11, 12)
PACE_EARLY = (0, 1, 3, 5, 7, 9, 13, 17, 19)


class Reduce:
    def __init__(self, at, part, g_ref, outs, fin_ref, cr, xr, yr, zr, sems):
        self.at, self.part, self.g, self.fin = at, part, g_ref, fin_ref
        self.up, self.down, self.small = outs
        self.cr, self.xr, self.yr, self.zr = cr, xr, yr, zr
        self.sems = sems
        self.start = 3072 * part
        self.half = 1536 + 256 * part
        self.quarter, self.piece_rows = self.half // 4, self.half // 16
        self.side = self.quarter // 2
        self.mine = self.start + at.core * self.half

    def rows(self, at, count):
        return pl.ds(pl.multiple_of(at, 16), count)

    def core_copy(self, b):
        at, (s, r) = self.at, self.sems[0]
        other = self.start + (1 - at.core) * self.half
        return remote(self.g.at[b, self.rows(other, self.half)], self.cr.at[b, pl.ds(self.start // 2, self.half)], s.at[self.part, b], r.at[self.part, b], at.sibling())

    def first_copy(self, b, n):
        at, (s, r) = self.at, self.sems[1]
        quarter, high, k = ((2, 0, 1), (2, 1, 3), (1, 1, 1), (3, 0, 3), (1, 0, 1), (3, 1, 3))[n]
        rows = self.rows(self.mine + ((at.f1 + quarter) % 4) * self.quarter + high * self.side, self.side)
        return remote(self.g.at[b, rows], self.xr.at[b, n, pl.ds(192 * self.part, self.side)], s.at[self.part, b, n], r.at[self.part, b, n], at.first(k)[1])

    def second_copy(self, b, k):
        at, (s, r) = self.at, self.sems[2]
        q, device = at.second(k)
        rows = self.rows(self.mine + at.f1 * self.quarter + q * self.piece_rows, self.piece_rows)
        return remote(self.g.at[b, rows], self.yr.at[b, k - 1, pl.ds(96 * self.part, self.piece_rows)], s.at[self.part, b, k - 1], r.at[self.part, b, k - 1], device)

    def piece(self):
        at = self.at
        return self.rows(self.mine + at.f1 * self.quarter + at.f2 * self.piece_rows, self.piece_rows)

    def z_copy(self, b, hi, source):
        at, (s, r) = self.at, self.sems[3]
        device = (b % 4, hi * 32 + at.d % 32)
        return remote(self.g.at[b, self.piece()], self.zr.at[b // 4, source, pl.ds(96 * self.part, self.piece_rows)], s.at[self.part, b, hi], r.at[self.part, b // 4, source], device)

    def back_second(self, l, k, arriving):
        at, (s, r) = self.at, self.sems[4]
        device = at.second(k)[1]
        q = at.second(4 - k)[0] if arriving else at.f2
        rows = self.fin.at[l, self.rows(self.mine + at.f1 * self.quarter + q * self.piece_rows, self.piece_rows)]
        return remote(rows, rows, s.at[self.part, l, k - 1], r.at[self.part, l, k - 1], device)

    def back_first(self, l, k, arriving):
        at, (s, r) = self.at, self.sems[5]
        device = at.first(k)[1]
        q = at.first(4 - k)[0] if arriving else at.f1
        rows = self.fin.at[l, self.rows(self.mine + q * self.quarter, self.quarter)]
        return remote(rows, rows, s.at[self.part, l, k - 1], r.at[self.part, l, k - 1], device)

    def back_core(self, l, core):
        at, (s, r) = self.at, self.sems[6]
        rows = self.fin.at[l, self.rows(self.start + core * self.half, self.half)]
        return remote(rows, rows, s.at[self.part, l], r.at[self.part, l], at.sibling())

    def stage0(self, b):
        self.core_copy(b).start()

    def stage1(self, b):
        self.core_copy(b).wait()
        add_rows(self.g, b, self.mine, self.half, [self.cr.at[b, pl.ds(self.start // 2, self.half)]])
        for n in range(4):
            self.first_copy(b, n).start()

    def stage2(self, b):
        at = self.at
        for n in range(2):
            self.first_copy(b, n).wait_recv()
            quarter, high = ((1, 0), (3, 1))[n]
            base = self.mine + ((at.f1 + quarter) % 4) * self.quarter + high * self.side
            add_rows(self.g, b, base, self.side, [self.xr.at[b, n, pl.ds(192 * self.part, self.side)]])
            self.first_copy(b, 4 + n).start()

    def stage3(self, b):
        at = self.at
        for n in range(6):
            self.first_copy(b, n).wait_send()
        for n in range(2, 6):
            self.first_copy(b, n).wait_recv()
        base = self.mine + at.f1 * self.quarter
        for high, (one, two) in enumerate(((3, 4), (2, 5))):
            add_rows(self.g, b, base + high * self.side, self.side, [self.xr.at[b, n, pl.ds(192 * self.part, self.side)] for n in (one, two)])
        for k in (2, 1, 3):
            self.second_copy(b, k).start()

    def stage4(self, b):
        at = self.at
        for k in (1, 2, 3):
            self.second_copy(b, k).wait()
        base = self.mine + at.f1 * self.quarter + at.f2 * self.piece_rows
        add_rows(self.g, b, base, self.piece_rows, [self.yr.at[b, k, pl.ds(96 * self.part, self.piece_rows)] for k in range(3)])
        for hi in range(2):
            @pl.when(at.z != hi * 4 + b % 4)
            def _():
                self.z_copy(b, hi, at.z).start()

    def stage5(self, b):
        at = self.at
        for hi in range(2):
            @pl.when(at.z != hi * 4 + b % 4)
            def _():
                self.z_copy(b, hi, at.z).wait_send()

        @pl.when(at.s == b % 4)
        def _():
            l = b // 4
            for k in range(1, 8):
                self.z_copy(b, 0, (at.z + k) % 8).wait_recv()
            rows = pl.ds(96 * self.part, self.piece_rows)
            self.zr[l, at.z, rows, :] = self.g[b, self.piece(), :]
            total = self.zr[l, 0, rows, :].astype(F32)
            for z in range(1, 8):
                total = total + self.zr[l, z, rows, :].astype(F32)
            self.fin[l, self.piece(), :] = total.astype(BF)
            for k in (2, 1, 3):
                self.back_second(l, k, False).start()

    def stage6(self, b):
        @pl.when(self.at.s == b % 4)
        def _():
            l = b // 4
            for k in (1, 2, 3):
                self.back_second(l, k, False).wait_send()
                self.back_second(l, k, True).wait_recv()
            for k in (2, 1, 3):
                self.back_first(l, k, False).start()

    def stage7(self, b):
        at = self.at

        @pl.when(at.s == b % 4)
        def _():
            l = b // 4
            for k in (1, 2, 3):
                self.back_first(l, k, False).wait_send()
                self.back_first(l, k, True).wait_recv()
            self.back_core(l, at.core).start()

    def stage8(self, b):
        at = self.at

        @pl.when(at.s == b % 4)
        def _():
            l = b // 4
            self.back_core(l, at.core).wait_send()
            self.back_core(l, 1 - at.core).wait_recv()
            if self.part == 0:
                return
            for t in range(10):
                lanes = slice(128 * t, 128 * t + 128)
                self.up[l, :, lanes] = self.fin[l, UP + C * t : UP + C * t + C, :]
                self.down[l, :, lanes] = self.fin[l, DOWN + C * t : DOWN + C * t + C, :]
            for t in range(3):
                self.small[l, :, 128 * t : 128 * t + 128] = self.fin[l, SMALL + 64 * t : SMALL + 64 * t + 64, :].astype(F32)

    def stages(self):
        return [self.stage0, self.stage1, self.stage2, self.stage3, self.stage4, self.stage5, self.stage6, self.stage7, self.stage8]


def pair(*shape):
    return [pltpu.SemaphoreType.DMA(shape), pltpu.SemaphoreType.DMA(shape)]


def reduce_scratch():
    buffers = [
        pltpu.VMEM((2, ROWS, 128), BF),
        pltpu.VMEM((NB, ROWS // 2, 128), BF),
        pltpu.VMEM((NB, 6, ROWS // 16, 128), BF),
        pltpu.VMEM((NB, 3, ROWS // 32, 128), BF),
        pltpu.VMEM((2, 8, ROWS // 32, 128), BF),
    ]
    sems = pair(2, NB) + pair(2, NB, 6) + pair(2, NB, 3)
    sems += [pltpu.SemaphoreType.DMA((2, NB, 2)), pltpu.SemaphoreType.DMA((2, 2, 8))]
    sems += pair(2, 2, 3) + pair(2, 2, 3) + pair(2, 2)
    return buffers + sems


def make_reduce(at, part, g_ref, outs, refs):
    sems = [tuple(refs[5 + 2 * i : 7 + 2 * i]) for i in range(7)]
    return Reduce(at, part, g_ref, outs, *refs[:5], sems)


WHALF, SHARE, PART = 3200, 1600, 400


class Gather:
    def __init__(self, at, w_ref, small_ref, sems):
        self.at, self.w, self.small_ref = at, w_ref, small_ref
        self.zs, self.ps, self.cs, self.small_zs, self.small_cs = sems

    def block(self, l, kind):
        return l * 4 + (self.at.s + (3, 1, 2)[kind]) % 4

    def share(self, core, color):
        return pl.multiple_of(core * WHALF + color * SHARE, 16)

    def along_z(self, l, b, kind, device):
        w = self.w.at[b, pl.ds(self.share(self.at.core, self.at.color), SHARE)]
        return remote(w, w, self.zs[0].at[l, kind], self.zs[1].at[l, kind], device)

    def small_along_z(self, l, b, kind, device):
        small = self.small_ref.at[b, pl.ds(pl.multiple_of(self.at.core * 32, 32), 32)]
        return remote(small, small, self.small_zs[0].at[l, kind], self.small_zs[1].at[l, kind], device)

    def in_plane(self, l, kind, side, color):
        at = self.at
        w = self.w.at[self.block(l, kind), pl.ds(pl.multiple_of(self.share(at.core, color) + side * PART, 16), PART)]
        return remote(w, w, self.ps[0].at[l, kind, side], self.ps[1].at[l, kind, side], at.beside(side))

    def to_sibling(self, l, kind, core, color, which):
        w = self.w.at[self.block(l, kind), pl.ds(self.share(core, color), SHARE)]
        return remote(w, w, self.cs[0].at[l, kind, which], self.cs[1].at[l, kind, which], self.at.sibling())

    def small_to_sibling(self, l, kind, core):
        small = self.small_ref.at[self.block(l, kind), pl.ds(pl.multiple_of(core * 32, 32), 32)]
        return remote(small, small, self.small_cs[0].at[l, kind], self.small_cs[1].at[l, kind], self.at.sibling())

    def begin(self, l):
        at = self.at
        for kind, k in ((0, 1), (1, -1)):
            self.small_along_z(l, l * 4 + at.s, kind, at.up_z(k)).start()
        for kind, k in ((0, 1), (1, -1)):
            self.along_z(l, l * 4 + at.s, kind, at.up_z(k)).start()

    def relay(self, l, copy):
        at = self.at
        for kind, k in ((0, -1), (1, 1)):
            b = self.block(l, kind)
            copy(l, b, kind, at.up_z(k)).wait_recv()

            @pl.when(at.core == 1 - kind)
            def _():
                copy(l, b, 2, at.up_z(-k)).start()

    def small_ones(self, l):
        at = self.at
        self.small_along_z(l, self.block(l, 2), 2, at.up_z(1)).wait_recv()
        self.small_to_sibling(l, 2, at.core).start()
        for kind in range(3):
            self.small_to_sibling(l, kind, 1 - at.core).wait_recv()

    def spread(self, l, kind):
        at = self.at
        for side in range(4):
            self.in_plane(l, kind, side, at.color).start()
        self.to_sibling(l, kind, at.core, at.color, 0).start()

    def near(self, l):
        self.relay(l, self.small_along_z)
        self.relay(l, self.along_z)
        for kind in range(2):
            self.small_to_sibling(l, kind, self.at.core).start()
            self.spread(l, kind)

    def close_plane(self, l, kind):
        at = self.at
        for side in range(4):
            self.in_plane(l, kind, side, 1 - at.color).wait_recv()
        self.to_sibling(l, kind, at.core, 1 - at.color, 1).start()

    def far(self, l):
        at = self.at
        self.along_z(l, self.block(l, 2), 2, at.up_z(1)).wait_recv()
        self.spread(l, 2)
        for kind in range(2):
            self.close_plane(l, kind)

    def last(self, l):
        at = self.at
        self.close_plane(l, 2)
        for kind in range(3):
            self.to_sibling(l, kind, 1 - at.core, at.color, 0).wait_recv()
            self.to_sibling(l, kind, 1 - at.core, 1 - at.color, 1).wait_recv()

    def drain(self, l):
        at = self.at
        for kind in range(3):
            self.along_z(l, self.block(l, kind), kind, at.up_z(1)).wait_send()
            self.small_along_z(l, self.block(l, kind), kind, at.up_z(1)).wait_send()
            for side in range(4):
                self.in_plane(l, kind, side, at.color).wait_send()
            self.to_sibling(l, kind, at.core, at.color, 0).wait_send()
            self.to_sibling(l, kind, at.core, 1 - at.color, 1).wait_send()
            self.small_to_sibling(l, kind, at.core).wait_send()


def gather_scratch():
    return pair(2, 3) + pair(2, 3, 4) + pair(2, 3, 2) + pair(2, 3) + pair(2, 3)


def make_gather(at, w_ref, small_ref, sems):
    return Gather(at, w_ref, small_ref, [tuple(sems[2 * i : 2 * i + 2]) for i in range(5)])


def clear(ref):
    ref[...] = jnp.zeros(ref.shape, ref.dtype)


def step_kernel(heights_ref, images_ref, cot_ref, up_in, down_in, small_in, up_out, down_out, small_out, w_ref, small_ref, image_ref, v_ref, pad_ref, shift_ref, mix_ref, x_ref, act_ref, slope_ref, xhat_ref, inv_ref, proj_ref, dk_ref, sg_ref, g_ref, load_sem, own_sem, *refs):
    at = Place()
    gather = make_gather(at, w_ref, small_ref, refs[:10])
    units = [make_reduce(at, part, w_ref, (up_out, down_out, small_out), refs[10:]) for part in range(2)]
    own = [[], []]
    for l in range(2):
        b = l * 4 + at.s
        for t in range(10):
            lanes = pl.ds(128 * t, 128)
            own[l].append(pltpu.make_async_copy(up_in.at[l, :, lanes], w_ref.at[b, pl.ds(UP + C * t, C)], own_sem.at[l, t]))
            own[l].append(pltpu.make_async_copy(down_in.at[l, :, lanes], w_ref.at[b, pl.ds(DOWN + C * t, C)], own_sem.at[l, 10 + t]))
        own[l].append(pltpu.make_async_copy(small_in.at[l], small_ref.at[b], own_sem.at[l, 20]))
    load = [pltpu.make_async_copy(images_ref.at[at.s, 0], image_ref.at[0], load_sem.at[0]), pltpu.make_async_copy(cot_ref.at[at.s, 0], image_ref.at[1], load_sem.at[1])]
    for c in own[0] + own[1] + load:
        c.start()
    greet([at.sibling()] + [at.first(k)[1] for k in (1, 2, 3)] + [at.second(k)[1] for k in (1, 2, 3)] + [at.up_z(k) for k in range(1, 8)])
    for c in own[0]:
        c.wait()
    gather.begin(0)
    clear(pad_ref)
    clear(x_ref)
    clear(sg_ref)
    h = heights_ref[at.s]
    for c in load + own[1]:
        c.wait()
    v_ref[0] = (image_ref[0].astype(F32).reshape(CELLS, C) * window_of(h)).astype(BF)
    gather.near(0)
    gather.begin(1)
    gather.small_ones(0)
    spatial_forward(0, small_ref, v_ref, pad_ref, shift_ref, mix_ref, xhat_ref, inv_ref)
    gather.far(0)
    gather.last(0)

    def forward(b, _):
        @pl.when(b > 0)
        def _():
            spatial_forward(b, small_ref, v_ref, pad_ref, shift_ref, mix_ref, xhat_ref, inv_ref)
        products_forward(b, h, w_ref, small_ref, v_ref, act_ref, slope_ref, xhat_ref, proj_ref)
        for n, part in ((0, gather.near), (2, gather.far), (2, gather.small_ones), (3, gather.last)):
            @pl.when(b == n)
            def _():
                part(1)
        return 0

    lax.fori_loop(0, NB, forward, 0)
    gather.drain(0)
    gather.drain(1)
    g_ref[...] = image_ref[1].astype(F32).reshape(CELLS, C)
    stages = [unit.stages() for unit in units]

    def run_stages(t, first):
        for n, (late, early) in enumerate(zip(PACE_LATE, PACE_EARLY)):
            spans = [(late, 0, NB)] if late == early else [(late, 0, NB // 2), (early, NB // 2, NB)]
            for ago, least, end in spans:
                b = NB - 1 - t - (first - ago) // 2

                @pl.when((b >= least) & (b < end))
                def _():
                    stages[(first - ago) % 2][n](b)

    def tick(t, _):
        b = NB - 1 - t

        @pl.when(b >= 0)
        def _():
            w_ref[b, ROWS - 64 : ROWS, :] = jnp.zeros((64, 128), BF)
            products_backward(b, h, g_ref, w_ref, small_ref, pad_ref, act_ref, slope_ref, xhat_ref, inv_ref, proj_ref, sg_ref)
        run_stages(t, 0)

        @pl.when(b >= 0)
        def _():
            spatial_backward(b, g_ref, w_ref, small_ref, v_ref, pad_ref, shift_ref, mix_ref, x_ref, dk_ref, sg_ref)
        run_stages(t, 1)
        return 0

    lax.fori_loop(0, max(2 * NB - 1 + PACE_LATE[-1], NB - 1 + PACE_EARLY[-1]) // 2 + 1, tick, 0)


def step(heights, images, cotangent, up, down, small):
    hbm = pl.BlockSpec(memory_space=pl.ANY)
    vm = pl.BlockSpec(memory_space=pltpu.VMEM)
    scratch = [
        pltpu.VMEM((NB, ROWS, 128), BF),
        pltpu.VMEM((NB, 64, CP), F32),
        pltpu.VMEM((2, SIDE, SIDE, C), BF),
        pltpu.VMEM((NB + 1, CELLS, C), BF),
        pltpu.VMEM((SIDE, 32, CP), F32),
        pltpu.VMEM((7, SIDE, SIDE, CP), F32),
        pltpu.VMEM((SIDE, SIDE, CP), F32),
        pltpu.VMEM((SIDE, SIDE, CP), F32),
        pltpu.VMEM((NB, CELLS, HID), BF),
        pltpu.VMEM((NB, CELLS, HID), BF),
        pltpu.VMEM((NB, CELLS, C), F32),
        pltpu.VMEM((NB, CELLS, 1), F32),
        pltpu.VMEM((NB, CELLS, C), BF),
        pltpu.VMEM((49, 8, CP), F32),
        pltpu.VMEM((64, CP), F32),
        pltpu.VMEM((CELLS, C), F32),
        pltpu.SemaphoreType.DMA((2,)),
        pltpu.SemaphoreType.DMA((2, 21)),
    ]
    return pl.pallas_call(
        step_kernel,
        out_shape=(jax.ShapeDtypeStruct((2, C, HID), BF), jax.ShapeDtypeStruct((2, C, HID), BF), jax.ShapeDtypeStruct((2, 64, CP), F32)),
        in_specs=[pl.BlockSpec(memory_space=pltpu.SMEM)] + [hbm] * 5,
        out_specs=(vm, vm, vm),
        scratch_shapes=scratch + gather_scratch() + reduce_scratch(),
        compiler_params=pltpu.CompilerParams(collective_id=0, has_side_effects=True, vmem_limit_bytes=62 * 2**20),
        cost_estimate=pl.CostEstimate(flops=12 * 10**9, bytes_accessed=30 * 10**6, transcendentals=3 * 10**6),
    )(heights, images, cotangent, up, down, small)


def body(images, cotangent, heights, dw_kernel, dw_bias, norm_gain, norm_bias, up_weight, up_bias, down_weight, down_bias, layer_scale):
    small = pack_small(*(a[:, 0] for a in (dw_kernel, dw_bias, norm_gain, norm_bias, up_bias, down_bias, layer_scale)))
    up, down, small = step(heights, images, cotangent, up_weight[:, 0], down_weight[:, 0].swapaxes(1, 2), small)
    row = lambda i: small[:, i, :C]
    up_bias_grad = small[:, 54:58].reshape(2, 4 * CP)[:, :HID]
    parts = (small[:, :49, :C].reshape(2, 7, 7, C), row(49), row(50), row(51), up, up_bias_grad, down.swapaxes(1, 2), row(52), row(53))
    return tuple(p[:, None] for p in parts)


def solution(mesh):
    three, two = P(None, "section", None, None), P(None, "section", None)
    five = P(None, "section", None, None, None)
    image = P(None, "dp", None, None, None)
    weights = (five, two, two, two, three, two, three, two, two)
    return jax.shard_map(body, mesh=mesh, in_specs=(image, image, P()) + weights, out_specs=weights, check_vma=False)
```

```python
import jax
import jax.numpy as jnp
from jax import lax
from jax.experimental import pallas as pl
from jax.experimental.pallas import tpu as pltpu
from jax.sharding import PartitionSpec as P

C, HID, SIDE, NB = 320, 1280, 16, 8
CP = 384
CELLS = SIDE * SIDE
ROWS = 6656
DOWN, UP, SMALL = 0, 3200, 6400
BF, F32 = jnp.bfloat16, jnp.float32
K0, K1 = 0.7978845608028654, 0.044715
T_LANES = (((1,), (1,)), ((), ()))
T_ROWS = (((0,), (0,)), ((), ()))


def dot(a, b, dims=(((1,), (0,)), ((), ()))):
    return lax.dot_general(a, b, dims, preferred_element_type=F32)


def lane_tile(t):
    return pl.ds(pl.multiple_of(t * 128, 128), 128)


def shift_columns(pad_ref, shift_ref, first, step):
    for dj in range(7):
        at = first + step * dj
        shift_ref[dj] = pad_ref[:, at : at + SIDE, :]


def taps_of(small_ref, b, dj, lanes):
    return [jnp.broadcast_to(small_ref[b, dr * 7 + dj : dr * 7 + dj + 1, lanes], (8, 128)) for dr in range(7)]


def conv_forward(shift_ref, small_ref, b, out_ref):
    def tile(t, _):
        lanes = lane_tile(t)
        for half in range(2):
            cols = pl.ds(8 * half, 8)
            acc = [jnp.broadcast_to(small_ref[b, 49:50, lanes], (8, 128))] * SIDE
            for dj in range(7):
                taps = taps_of(small_ref, b, dj, lanes)
                for r in range(SIDE):
                    x = shift_ref[dj, r, cols, lanes]
                    for dr in range(7):
                        i = r - dr + 3
                        if 0 <= i < SIDE:
                            acc[i] = acc[i] + x * taps[dr]
            for i in range(SIDE):
                out_ref[i, cols, lanes] = acc[i]
        return 0

    lax.fori_loop(0, 3, tile, 0)


def conv_backward(shift_ref, x_ref, small_ref, b, dx_ref, dk_ref, inputs):
    def tile(t, _):
        lanes = lane_tile(t)
        for half in range(2):
            cols = pl.ds(8 * half, 8)
            xs = [x_ref[i, cols, lanes] for i in range(SIDE)]
            acc = [None] * SIDE
            for dj in range(7):
                taps = taps_of(small_ref, b, dj, lanes)
                dks = [None] * 7
                for r in range(SIDE):
                    g = shift_ref[dj, r, cols, lanes]
                    for dr in range(7):
                        i = r + dr - 3
                        if 0 <= i < SIDE:
                            if inputs:
                                p = g * taps[dr]
                                acc[i] = p if acc[i] is None else acc[i] + p
                            p = g * xs[i]
                            dks[dr] = p if dks[dr] is None else dks[dr] + p
                for dr in range(7):
                    if half == 0:
                        dk_ref[dr * 7 + dj, :, lanes] = dks[dr]
                    else:
                        dk_ref[dr * 7 + dj, :, lanes] += dks[dr]
            for i in range(SIDE if inputs else 0):
                dx_ref[i, cols, lanes] = acc[i]
        return 0

    lax.fori_loop(0, 3, tile, 0)


def weight_chunk(w_ref, b, base, n):
    at = base + 640 * n
    return jnp.concatenate([w_ref[b, at : at + C, :], w_ref[b, at + C : at + 2 * C, :]], axis=1)


def small_row(small_ref, b, row):
    return small_ref[b, row : row + 1, 0:C]


def up_bias_chunk(small_ref, b, n):
    parts = []
    for t in (2 * n, 2 * n + 1):
        parts.append(small_ref[b, 54 + t // 3 : 55 + t // 3, (t % 3) * 128 : (t % 3 + 1) * 128])
    return jnp.concatenate(parts, axis=1)


def window_of(h):
    cell = lax.broadcasted_iota(jnp.int32, (CELLS, 1), 0)
    return ((cell // SIDE < h) & (cell % SIDE < h)).astype(F32)


def spatial_forward(b, small_ref, v_ref, pad_ref, shift_ref, mix_ref, xhat_ref, inv_ref):
    pad_ref[:, 8:24, 0:C] = v_ref[b].astype(F32).reshape(SIDE, SIDE, C)
    shift_columns(pad_ref, shift_ref, 5, 1)
    conv_forward(shift_ref, small_ref, b, mix_ref)
    mixed = mix_ref[:, :, 0:C].reshape(CELLS, C)
    center = jnp.sum(mixed, axis=1, keepdims=True) * (1.0 / C)
    mixed = mixed - center
    inv = lax.rsqrt(jnp.sum(mixed * mixed, axis=1, keepdims=True) * (1.0 / C) + 1e-6)
    xhat_ref[b] = mixed * inv
    inv_ref[b] = inv


def products_forward(b, h, w_ref, small_ref, v_ref, act_ref, slope_ref, xhat_ref, proj_ref):
    xhat = xhat_ref[b]
    normed = (xhat * small_row(small_ref, b, 50) + small_row(small_ref, b, 51)).astype(BF)
    proj = jnp.broadcast_to(small_row(small_ref, b, 52), (CELLS, C))
    for n in range(5):
        cols = slice(256 * n, 256 * n + 256)
        u = dot(normed, weight_chunk(w_ref, b, UP, n)) + up_bias_chunk(small_ref, b, n)
        uu = u * u
        t = jnp.tanh(u * (K0 + (K0 * K1) * uu))
        lift = 0.5 + 0.5 * t
        act = (u * lift).astype(BF)
        slope = lift + (u * (0.5 - 0.5 * t * t)) * (K0 + (3 * K0 * K1) * uu)
        act_ref[b, :, cols] = act
        slope_ref[b, :, cols] = slope.astype(BF)
        proj = proj + dot(act, weight_chunk(w_ref, b, DOWN, n), T_LANES)
    proj_ref[b] = proj.astype(BF)
    out = (v_ref[b].astype(F32) + small_row(small_ref, b, 53) * proj) * window_of(h)
    v_ref[b + 1] = out.astype(BF)


def products_backward(b, h, g_ref, w_ref, small_ref, pad_ref, act_ref, slope_ref, xhat_ref, inv_ref, proj_ref, sg_ref):
    g = g_ref[...] * window_of(h)
    g_ref[...] = g
    sg_ref[53:54, 0:C] = jnp.sum(g * proj_ref[b].astype(F32), axis=0, keepdims=True)
    dproj = g * small_row(small_ref, b, 53)
    sg_ref[52:53, 0:C] = jnp.sum(dproj, axis=0, keepdims=True)
    dproj = dproj.astype(BF)
    xhat = xhat_ref[b]
    gain = small_row(small_ref, b, 50)
    normed = (xhat * gain + small_row(small_ref, b, 51)).astype(BF)
    dnormed = None
    for n in range(5):
        cols = slice(256 * n, 256 * n + 256)
        dact = dot(dproj, weight_chunk(w_ref, b, DOWN, n))
        dhid = dact * slope_ref[b, :, cols].astype(F32)
        bias = jnp.sum(dhid, axis=0, keepdims=True)
        dhid = dhid.astype(BF)
        part = dot(dhid, weight_chunk(w_ref, b, UP, n), T_LANES)
        dnormed = part if dnormed is None else dnormed + part
        dup = dot(normed, dhid, T_ROWS).astype(BF)
        ddown = dot(dproj, act_ref[b, :, cols], T_ROWS).astype(BF)
        for k in range(2):
            t = 2 * n + k
            lanes = slice(128 * k, 128 * k + 128)
            w_ref[b, UP + C * t : UP + C * t + C, :] = dup[:, lanes]
            w_ref[b, DOWN + C * t : DOWN + C * t + C, :] = ddown[:, lanes]
            sg_ref[54 + t // 3 : 55 + t // 3, (t % 3) * 128 : (t % 3 + 1) * 128] = bias[:, lanes]
    sg_ref[50:51, 0:C] = jnp.sum(dnormed * xhat, axis=0, keepdims=True)
    sg_ref[51:52, 0:C] = jnp.sum(dnormed, axis=0, keepdims=True)
    dxhat = dnormed * gain
    m0 = jnp.sum(dxhat, axis=1, keepdims=True) * (1.0 / C)
    m1 = jnp.sum(dxhat * xhat, axis=1, keepdims=True) * (1.0 / C)
    dmixed = inv_ref[b] * (dxhat - m0 - xhat * m1)
    sg_ref[49:50, 0:C] = jnp.sum(dmixed, axis=0, keepdims=True)
    pad_ref[:, 8:24, 0:C] = dmixed.reshape(SIDE, SIDE, C)


def spatial_backward(b, g_ref, w_ref, small_ref, v_ref, pad_ref, shift_ref, mix_ref, x_ref, dk_ref, sg_ref, inputs):
    x_ref[:, :, 0:C] = v_ref[b].astype(F32).reshape(SIDE, SIDE, C)
    shift_columns(pad_ref, shift_ref, 11, -1)
    conv_backward(shift_ref, x_ref, small_ref, b, mix_ref, dk_ref, inputs)
    sg_ref[0:49, :] = jnp.sum(dk_ref[...], axis=1)
    for j in range(3):
        w_ref[b, SMALL + 64 * j : SMALL + 64 * j + 64, :] = sg_ref[:, 128 * j : 128 * j + 128].astype(BF)
    if inputs:
        g_ref[...] = (g_ref[...] + mix_ref[:, :, 0:C].reshape(CELLS, C)).astype(BF).astype(F32)


def pack_small(dw_kernel, dw_bias, gain, nbias, up_bias, down_bias, scale):
    n = dw_kernel.shape[0]
    rows = jnp.concatenate([dw_kernel.reshape(n, 49, C), dw_bias[:, None], gain[:, None], nbias[:, None], down_bias[:, None], scale[:, None]], axis=1)
    rows = jnp.pad(rows, ((0, 0), (0, 0), (0, CP - C)))
    up = jnp.pad(up_bias, ((0, 0), (0, 4 * CP - HID))).reshape(n, 4, CP)
    return jnp.concatenate([rows, up, jnp.zeros((n, 6, CP), F32)], axis=1)


MESH = pl.DeviceIdType.MESH


class Place:
    def __init__(self):
        s, d = lax.axis_index("section"), lax.axis_index("dp")
        self.s, self.d = s, d
        self.core = d % 2
        self.z = (d // 32) * 4 + s
        self.step1 = 2 + 6 * self.core
        self.step2 = 10 - self.step1
        self.f1 = (d // self.step1) % 4
        self.f2 = (d // self.step2) % 4
        self.x, self.y = (d // 2) % 4, (d // 8) % 4
        self.color = (self.x + self.y) % 2

    def sibling(self):
        return (self.s, self.d + 1 - 2 * self.core)

    def first(self, k):
        q = (self.f1 + k) % 4
        return q, (self.s, self.d + (q - self.f1) * self.step1)

    def second(self, k):
        q = (self.f2 + k) % 4
        return q, (self.s, self.d + (q - self.f2) * self.step2)

    def beside(self, side):
        step, at = (2, self.x) if side < 2 else (8, self.y)
        k = 1 if side % 2 == 0 else 3
        return (self.s, self.d + ((at + k) % 4 - at) * step)

    def up_z(self, k):
        z = (self.z + k) % 8
        return (z % 4, (z // 4) * 32 + self.d % 32)


def greet(devices):
    barrier = pltpu.get_barrier_semaphore()
    for device in devices:
        pl.semaphore_signal(barrier, inc=1, device_id=device, device_id_type=MESH)
    pl.semaphore_wait(barrier, len(devices))


def remote(src, dst, send, recv, device):
    return pltpu.make_async_remote_copy(src_ref=src, dst_ref=dst, send_sem=send, recv_sem=recv, device_id=device, device_id_type=MESH)


def add_rows(dst_ref, b, base, count, src_refs):
    step = next(n for n in (256, 224, 208, 192, 112, 96) if count % n == 0)

    def add(i, _):
        rows = pl.ds(pl.multiple_of(base + i * step, 16), step)
        own = pl.ds(pl.multiple_of(i * step, 16), step)
        total = dst_ref[b, rows, :].astype(F32)
        for src in src_refs:
            total = total + src[own, :].astype(F32)
        dst_ref[b, rows, :] = total.astype(BF)
        return 0

    lax.fori_loop(0, count // step, add, 0)


PACE_LATE = (0, 1, 3, 5, 7, 9, 10, 11, 12)
PACE_EARLY = (0, 1, 3, 5, 7, 9, 13, 17, 19)


class Reduce:
    def __init__(self, at, part, g_ref, outs, fin_ref, cr, xr, yr, zr, sems):
        self.at, self.part, self.g, self.fin = at, part, g_ref, fin_ref
        self.up, self.down, self.small = outs
        self.cr, self.xr, self.yr, self.zr = cr, xr, yr, zr
        self.sems = sems
        self.start = 3072 * part
        self.half = 1536 + 256 * part
        self.quarter, self.piece_rows = self.half // 4, self.half // 16
        self.side = self.quarter // 2
        self.mine = self.start + at.core * self.half

    def rows(self, at, count):
        return pl.ds(pl.multiple_of(at, 16), count)

    def core_copy(self, b):
        at, (s, r) = self.at, self.sems[0]
        other = self.start + (1 - at.core) * self.half
        return remote(self.g.at[b, self.rows(other, self.half)], self.cr.at[b, pl.ds(self.start // 2, self.half)], s.at[self.part, b], r.at[self.part, b], at.sibling())

    def first_copy(self, b, n):
        at, (s, r) = self.at, self.sems[1]
        quarter, high, k = ((2, 0, 1), (2, 1, 3), (1, 1, 1), (3, 0, 3), (1, 0, 1), (3, 1, 3))[n]
        rows = self.rows(self.mine + ((at.f1 + quarter) % 4) * self.quarter + high * self.side, self.side)
        return remote(self.g.at[b, rows], self.xr.at[b, n, pl.ds(192 * self.part, self.side)], s.at[self.part, b, n], r.at[self.part, b, n], at.first(k)[1])

    def second_copy(self, b, k):
        at, (s, r) = self.at, self.sems[2]
        q, device = at.second(k)
        rows = self.rows(self.mine + at.f1 * self.quarter + q * self.piece_rows, self.piece_rows)
        return remote(self.g.at[b, rows], self.yr.at[b, k - 1, pl.ds(96 * self.part, self.piece_rows)], s.at[self.part, b, k - 1], r.at[self.part, b, k - 1], device)

    def piece(self):
        at = self.at
        return self.rows(self.mine + at.f1 * self.quarter + at.f2 * self.piece_rows, self.piece_rows)

    def z_copy(self, b, hi, source):
        at, (s, r) = self.at, self.sems[3]
        device = (b % 4, hi * 32 + at.d % 32)
        return remote(self.g.at[b, self.piece()], self.zr.at[b // 4, source, pl.ds(96 * self.part, self.piece_rows)], s.at[self.part, b, hi], r.at[self.part, b // 4, source], device)

    def back_second(self, l, k, arriving):
        at, (s, r) = self.at, self.sems[4]
        device = at.second(k)[1]
        q = at.second(4 - k)[0] if arriving else at.f2
        rows = self.fin.at[l, self.rows(self.mine + at.f1 * self.quarter + q * self.piece_rows, self.piece_rows)]
        return remote(rows, rows, s.at[self.part, l, k - 1], r.at[self.part, l, k - 1], device)

    def back_first(self, l, k, arriving):
        at, (s, r) = self.at, self.sems[5]
        device = at.first(k)[1]
        q = at.first(4 - k)[0] if arriving else at.f1
        rows = self.fin.at[l, self.rows(self.mine + q * self.quarter, self.quarter)]
        return remote(rows, rows, s.at[self.part, l, k - 1], r.at[self.part, l, k - 1], device)

    def back_core(self, l, core):
        at, (s, r) = self.at, self.sems[6]
        rows = self.fin.at[l, self.rows(self.start + core * self.half, self.half)]
        return remote(rows, rows, s.at[self.part, l], r.at[self.part, l], at.sibling())

    def stage0(self, b):
        self.core_copy(b).start()

    def stage1(self, b):
        self.core_copy(b).wait()
        add_rows(self.g, b, self.mine, self.half, [self.cr.at[b, pl.ds(self.start // 2, self.half)]])
        for n in range(4):
            self.first_copy(b, n).start()

    def stage2(self, b):
        at = self.at
        for n in range(2):
            self.first_copy(b, n).wait_recv()
            quarter, high = ((1, 0), (3, 1))[n]
            base = self.mine + ((at.f1 + quarter) % 4) * self.quarter + high * self.side
            add_rows(self.g, b, base, self.side, [self.xr.at[b, n, pl.ds(192 * self.part, self.side)]])
            self.first_copy(b, 4 + n).start()

    def stage3(self, b):
        at = self.at
        for n in range(6):
            self.first_copy(b, n).wait_send()
        for n in range(2, 6):
            self.first_copy(b, n).wait_recv()
        base = self.mine + at.f1 * self.quarter
        for high, (one, two) in enumerate(((3, 4), (2, 5))):
            add_rows(self.g, b, base + high * self.side, self.side, [self.xr.at[b, n, pl.ds(192 * self.part, self.side)] for n in (one, two)])
        for k in (2, 1, 3):
            self.second_copy(b, k).start()

    def stage4(self, b):
        at = self.at
        for k in (1, 2, 3):
            self.second_copy(b, k).wait()
        base = self.mine + at.f1 * self.quarter + at.f2 * self.piece_rows
        add_rows(self.g, b, base, self.piece_rows, [self.yr.at[b, k, pl.ds(96 * self.part, self.piece_rows)] for k in range(3)])
        for hi in range(2):
            @pl.when(at.z != hi * 4 + b % 4)
            def _():
                self.z_copy(b, hi, at.z).start()

    def stage5(self, b):
        at = self.at
        for hi in range(2):
            @pl.when(at.z != hi * 4 + b % 4)
            def _():
                self.z_copy(b, hi, at.z).wait_send()

        @pl.when(at.s == b % 4)
        def _():
            l = b // 4
            for k in range(1, 8):
                self.z_copy(b, 0, (at.z + k) % 8).wait_recv()
            rows = pl.ds(96 * self.part, self.piece_rows)
            self.zr[l, at.z, rows, :] = self.g[b, self.piece(), :]
            total = self.zr[l, 0, rows, :].astype(F32)
            for z in range(1, 8):
                total = total + self.zr[l, z, rows, :].astype(F32)
            self.fin[l, self.piece(), :] = total.astype(BF)
            for k in (2, 1, 3):
                self.back_second(l, k, False).start()

    def stage6(self, b):
        @pl.when(self.at.s == b % 4)
        def _():
            l = b // 4
            for k in (1, 2, 3):
                self.back_second(l, k, False).wait_send()
                self.back_second(l, k, True).wait_recv()
            for k in (2, 1, 3):
                self.back_first(l, k, False).start()

    def stage7(self, b):
        at = self.at

        @pl.when(at.s == b % 4)
        def _():
            l = b // 4
            for k in (1, 2, 3):
                self.back_first(l, k, False).wait_send()
                self.back_first(l, k, True).wait_recv()
            self.back_core(l, at.core).start()

    def stage8(self, b):
        at = self.at

        @pl.when(at.s == b % 4)
        def _():
            l = b // 4
            self.back_core(l, at.core).wait_send()
            self.back_core(l, 1 - at.core).wait_recv()
            if self.part == 0:
                return
            for t in range(10):
                lanes = slice(128 * t, 128 * t + 128)
                self.up[l, :, lanes] = self.fin[l, UP + C * t : UP + C * t + C, :]
                self.down[l, :, lanes] = self.fin[l, DOWN + C * t : DOWN + C * t + C, :]
            for t in range(3):
                self.small[l, :, 128 * t : 128 * t + 128] = self.fin[l, SMALL + 64 * t : SMALL + 64 * t + 64, :].astype(F32)

    def stages(self):
        return [self.stage0, self.stage1, self.stage2, self.stage3, self.stage4, self.stage5, self.stage6, self.stage7, self.stage8]


def pair(*shape):
    return [pltpu.SemaphoreType.DMA(shape), pltpu.SemaphoreType.DMA(shape)]


def reduce_scratch():
    buffers = [
        pltpu.VMEM((2, ROWS, 128), BF),
        pltpu.VMEM((NB, ROWS // 2, 128), BF),
        pltpu.VMEM((NB, 6, ROWS // 16, 128), BF),
        pltpu.VMEM((NB, 3, ROWS // 32, 128), BF),
        pltpu.VMEM((2, 8, ROWS // 32, 128), BF),
    ]
    sems = pair(2, NB) + pair(2, NB, 6) + pair(2, NB, 3)
    sems += [pltpu.SemaphoreType.DMA((2, NB, 2)), pltpu.SemaphoreType.DMA((2, 2, 8))]
    sems += pair(2, 2, 3) + pair(2, 2, 3) + pair(2, 2)
    return buffers + sems


def make_reduce(at, part, g_ref, outs, refs):
    sems = [tuple(refs[5 + 2 * i : 7 + 2 * i]) for i in range(7)]
    return Reduce(at, part, g_ref, outs, *refs[:5], sems)


WHALF, SHARE, PART = 3200, 1600, 400


class Gather:
    def __init__(self, at, w_ref, small_ref, sems):
        self.at, self.w, self.small_ref = at, w_ref, small_ref
        self.zs, self.ps, self.cs, self.small_zs, self.small_cs = sems

    def block(self, l, kind):
        return l * 4 + (self.at.s + (3, 1, 2)[kind]) % 4

    def share(self, core, color):
        return pl.multiple_of(core * WHALF + color * SHARE, 16)

    def along_z(self, l, b, kind, device):
        w = self.w.at[b, pl.ds(self.share(self.at.core, self.at.color), SHARE)]
        return remote(w, w, self.zs[0].at[l, kind], self.zs[1].at[l, kind], device)

    def small_along_z(self, l, b, kind, device):
        small = self.small_ref.at[b, pl.ds(pl.multiple_of(self.at.core * 32, 32), 32)]
        return remote(small, small, self.small_zs[0].at[l, kind], self.small_zs[1].at[l, kind], device)

    def in_plane(self, l, kind, side, color):
        at = self.at
        w = self.w.at[self.block(l, kind), pl.ds(pl.multiple_of(self.share(at.core, color) + side * PART, 16), PART)]
        return remote(w, w, self.ps[0].at[l, kind, side], self.ps[1].at[l, kind, side], at.beside(side))

    def to_sibling(self, l, kind, core, color, which):
        w = self.w.at[self.block(l, kind), pl.ds(self.share(core, color), SHARE)]
        return remote(w, w, self.cs[0].at[l, kind, which], self.cs[1].at[l, kind, which], self.at.sibling())

    def small_to_sibling(self, l, kind, core):
        small = self.small_ref.at[self.block(l, kind), pl.ds(pl.multiple_of(core * 32, 32), 32)]
        return remote(small, small, self.small_cs[0].at[l, kind], self.small_cs[1].at[l, kind], self.at.sibling())

    def begin(self, l):
        at = self.at
        for kind, k in ((0, 1), (1, -1)):
            self.small_along_z(l, l * 4 + at.s, kind, at.up_z(k)).start()
        for kind, k in ((0, 1), (1, -1)):
            self.along_z(l, l * 4 + at.s, kind, at.up_z(k)).start()

    def relay(self, l, copy):
        at = self.at
        for kind, k in ((0, -1), (1, 1)):
            b = self.block(l, kind)
            copy(l, b, kind, at.up_z(k)).wait_recv()

            @pl.when(at.core == 1 - kind)
            def _():
                copy(l, b, 2, at.up_z(-k)).start()

    def small_ones(self, l):
        at = self.at
        self.small_along_z(l, self.block(l, 2), 2, at.up_z(1)).wait_recv()
        self.small_to_sibling(l, 2, at.core).start()
        for kind in range(3):
            self.small_to_sibling(l, kind, 1 - at.core).wait_recv()

    def spread(self, l, kind):
        at = self.at
        for side in range(4):
            self.in_plane(l, kind, side, at.color).start()
        self.to_sibling(l, kind, at.core, at.color, 0).start()

    def near(self, l):
        self.relay(l, self.small_along_z)
        self.relay(l, self.along_z)
        for kind in range(2):
            self.small_to_sibling(l, kind, self.at.core).start()
            self.spread(l, kind)

    def close_plane(self, l, kind):
        at = self.at
        for side in range(4):
            self.in_plane(l, kind, side, 1 - at.color).wait_recv()
        self.to_sibling(l, kind, at.core, 1 - at.color, 1).start()

    def far(self, l):
        at = self.at
        self.along_z(l, self.block(l, 2), 2, at.up_z(1)).wait_recv()
        self.spread(l, 2)
        for kind in range(2):
            self.close_plane(l, kind)

    def last(self, l):
        at = self.at
        self.close_plane(l, 2)
        for kind in range(3):
            self.to_sibling(l, kind, 1 - at.core, at.color, 0).wait_recv()
            self.to_sibling(l, kind, 1 - at.core, 1 - at.color, 1).wait_recv()

    def drain(self, l):
        at = self.at
        for kind in range(3):
            self.along_z(l, self.block(l, kind), kind, at.up_z(1)).wait_send()
            self.small_along_z(l, self.block(l, kind), kind, at.up_z(1)).wait_send()
            for side in range(4):
                self.in_plane(l, kind, side, at.color).wait_send()
            self.to_sibling(l, kind, at.core, at.color, 0).wait_send()
            self.to_sibling(l, kind, at.core, 1 - at.color, 1).wait_send()
            self.small_to_sibling(l, kind, at.core).wait_send()


def gather_scratch():
    return pair(2, 3) + pair(2, 3, 4) + pair(2, 3, 2) + pair(2, 3) + pair(2, 3)


def make_gather(at, w_ref, small_ref, sems):
    return Gather(at, w_ref, small_ref, [tuple(sems[2 * i : 2 * i + 2]) for i in range(5)])


def clear(ref):
    ref[...] = jnp.zeros(ref.shape, ref.dtype)


def step_kernel(heights_ref, images_ref, cot_ref, up_in, down_in, small_in, up_out, down_out, small_out, w_ref, small_ref, image_ref, v_ref, pad_ref, shift_ref, mix_ref, x_ref, act_ref, slope_ref, xhat_ref, inv_ref, proj_ref, dk_ref, sg_ref, g_ref, load_sem, own_sem, *refs):
    at = Place()
    gather = make_gather(at, w_ref, small_ref, refs[:10])
    units = [make_reduce(at, part, w_ref, (up_out, down_out, small_out), refs[10:]) for part in range(2)]
    own = [[], []]
    for l in range(2):
        b = l * 4 + at.s
        for t in range(10):
            lanes = pl.ds(128 * t, 128)
            own[l].append(pltpu.make_async_copy(up_in.at[l, :, lanes], w_ref.at[b, pl.ds(UP + C * t, C)], own_sem.at[l, t]))
            own[l].append(pltpu.make_async_copy(down_in.at[l, :, lanes], w_ref.at[b, pl.ds(DOWN + C * t, C)], own_sem.at[l, 10 + t]))
        own[l].append(pltpu.make_async_copy(small_in.at[l], small_ref.at[b], own_sem.at[l, 20]))
    load = [pltpu.make_async_copy(images_ref.at[at.s, 0], image_ref.at[0], load_sem.at[0]), pltpu.make_async_copy(cot_ref.at[at.s, 0], image_ref.at[1], load_sem.at[1])]
    for c in own[0] + own[1] + load:
        c.start()
    greet([at.sibling()] + [at.first(k)[1] for k in (1, 2, 3)] + [at.second(k)[1] for k in (1, 2, 3)] + [at.up_z(k) for k in range(1, 8)])
    for c in own[0]:
        c.wait()
    gather.begin(0)
    clear(pad_ref)
    clear(x_ref)
    clear(sg_ref)
    h = heights_ref[at.s]
    for c in load + own[1]:
        c.wait()
    v_ref[0] = (image_ref[0].astype(F32).reshape(CELLS, C) * window_of(h)).astype(BF)
    gather.near(0)
    gather.small_ones(0)
    spatial_forward(0, small_ref, v_ref, pad_ref, shift_ref, mix_ref, xhat_ref, inv_ref)
    gather.far(0)
    gather.begin(1)
    gather.last(0)

    def forward(b, _):
        @pl.when(b > 0)
        def _():
            spatial_forward(b, small_ref, v_ref, pad_ref, shift_ref, mix_ref, xhat_ref, inv_ref)
        products_forward(b, h, w_ref, small_ref, v_ref, act_ref, slope_ref, xhat_ref, proj_ref)
        for n, part in ((1, gather.near), (3, gather.far), (3, gather.small_ones), (3, gather.last)):
            @pl.when(b == n)
            def _():
                part(1)
        return 0

    lax.fori_loop(0, NB, forward, 0)
    gather.drain(0)
    gather.drain(1)
    g_ref[...] = image_ref[1].astype(F32).reshape(CELLS, C)
    stages = [unit.stages() for unit in units]

    def run_stages(t, first):
        for n, (late, early) in enumerate(zip(PACE_LATE, PACE_EARLY)):
            spans = [(late, 0, NB)] if late == early else [(late, 0, NB // 2), (early, NB // 2, NB)]
            for ago, least, end in spans:
                b = NB - 1 - t - (first - ago) // 2

                @pl.when((b >= least) & (b < end))
                def _():
                    stages[(first - ago) % 2][n](b)

    def tick(t, _):
        b = NB - 1 - t

        @pl.when(b >= 0)
        def _():
            w_ref[b, ROWS - 64 : ROWS, :] = jnp.zeros((64, 128), BF)
            products_backward(b, h, g_ref, w_ref, small_ref, pad_ref, act_ref, slope_ref, xhat_ref, inv_ref, proj_ref, sg_ref)
        run_stages(t, 0)

        @pl.when(b > 0)
        def _():
            spatial_backward(b, g_ref, w_ref, small_ref, v_ref, pad_ref, shift_ref, mix_ref, x_ref, dk_ref, sg_ref, True)

        @pl.when(b == 0)
        def _():
            spatial_backward(0, g_ref, w_ref, small_ref, v_ref, pad_ref, shift_ref, mix_ref, x_ref, dk_ref, sg_ref, False)
        run_stages(t, 1)
        return 0

    lax.fori_loop(0, max(2 * NB - 1 + PACE_LATE[-1], NB - 1 + PACE_EARLY[-1]) // 2 + 1, tick, 0)


def step(heights, images, cotangent, up, down, small):
    hbm = pl.BlockSpec(memory_space=pl.ANY)
    vm = pl.BlockSpec(memory_space=pltpu.VMEM)
    scratch = [
        pltpu.VMEM((NB, ROWS, 128), BF),
        pltpu.VMEM((NB, 64, CP), F32),
        pltpu.VMEM((2, SIDE, SIDE, C), BF),
        pltpu.VMEM((NB + 1, CELLS, C), BF),
        pltpu.VMEM((SIDE, 32, CP), F32),
        pltpu.VMEM((7, SIDE, SIDE, CP), F32),
        pltpu.VMEM((SIDE, SIDE, CP), F32),
        pltpu.VMEM((SIDE, SIDE, CP), F32),
        pltpu.VMEM((NB, CELLS, HID), BF),
        pltpu.VMEM((NB, CELLS, HID), BF),
        pltpu.VMEM((NB, CELLS, C), F32),
        pltpu.VMEM((NB, CELLS, 1), F32),
        pltpu.VMEM((NB, CELLS, C), BF),
        pltpu.VMEM((49, 8, CP), F32),
        pltpu.VMEM((64, CP), F32),
        pltpu.VMEM((CELLS, C), F32),
        pltpu.SemaphoreType.DMA((2,)),
        pltpu.SemaphoreType.DMA((2, 21)),
    ]
    return pl.pallas_call(
        step_kernel,
        out_shape=(jax.ShapeDtypeStruct((2, C, HID), BF), jax.ShapeDtypeStruct((2, C, HID), BF), jax.ShapeDtypeStruct((2, 64, CP), F32)),
        in_specs=[pl.BlockSpec(memory_space=pltpu.SMEM)] + [hbm] * 5,
        out_specs=(vm, vm, vm),
        scratch_shapes=scratch + gather_scratch() + reduce_scratch(),
        compiler_params=pltpu.CompilerParams(collective_id=0, has_side_effects=True, vmem_limit_bytes=62 * 2**20),
        cost_estimate=pl.CostEstimate(flops=12 * 10**9, bytes_accessed=30 * 10**6, transcendentals=3 * 10**6),
    )(heights, images, cotangent, up, down, small)


def body(images, cotangent, heights, dw_kernel, dw_bias, norm_gain, norm_bias, up_weight, up_bias, down_weight, down_bias, layer_scale):
    small = pack_small(*(a[:, 0] for a in (dw_kernel, dw_bias, norm_gain, norm_bias, up_bias, down_bias, layer_scale)))
    up, down, small = step(heights, images, cotangent, up_weight[:, 0], down_weight[:, 0].swapaxes(1, 2), small)
    row = lambda i: small[:, i, :C]
    up_bias_grad = small[:, 54:58].reshape(2, 4 * CP)[:, :HID]
    parts = (small[:, :49, :C].reshape(2, 7, 7, C), row(49), row(50), row(51), up, up_bias_grad, down.swapaxes(1, 2), row(52), row(53))
    return tuple(p[:, None] for p in parts)


def solution(mesh):
    three, two = P(None, "section", None, None), P(None, "section", None)
    five = P(None, "section", None, None, None)
    image = P(None, "dp", None, None, None)
    weights = (five, two, two, two, three, two, three, two, two)
    return jax.shard_map(body, mesh=mesh, in_specs=(image, image, P()) + weights, out_specs=weights, check_vma=False)
```
